768 devices in a mesh: aux: 48 (over x, z), orb: 16 (over y, core).
Axes of the slice: x: 4, y: 8, z: 12, core: 2. Of those that a mesh axis runs over, the one named last changes fastest.
Arguments:
- three_centre: bfloat16 [192, 2048, 2048], P('aux', 'orb'), may hold values from -0.125 to 0.125
- screening: int32 [192, 16, 16], P('aux', 'orb'), may hold values 0 or 1
- coefficients: bfloat16 [2048, 768], replicated, may hold values from -0.015625 to 0.015625
- occ_pattern: int32 [16, 48], replicated, may hold values 0 or 1
Outputs:
- exchange_matrix: float32 [2048, 2048], P('orb')
The draws below stay inside these ranges and needn't reach their ends.
All inputs are finite; a program needn't handle non-finite values. No bound on the sum of `screening` on one device may be relied on, other than what follows from the above.
Results may differ from the reference program's by a relative error of at most 0.0015.
Values may be sent and summed in bfloat16 or wider, within the bound.
A program may use at most 64 MiB of HBM per device.

```python
import jax
import jax.numpy as jnp
from jax import lax

OBS = 128
OCC_DEV = 16
NAUX = 192
OCC_BLOCKS = 48
NOCC = 768
NOB = 16
NORB = 2048


def with_ends(entries, rng, low, top_value):
    dims = entries.shape
    spot = [jax.random.randint(jax.random.fold_in(rng, axis), (), 0, dims[axis]) for axis in range(len(dims))]
    entries = entries.at[tuple(spot)].set(low)
    longest = dims.index(max(dims))
    spot[longest] = (spot[longest] + 1) % dims[longest]
    return entries.at[tuple(spot)].set(top_value)


def block_levels(stream_key, shape, shards, low, largest):
    def one(axis_at, blocks):
        draws = jax.random.uniform(jax.random.fold_in(jax.random.fold_in(stream_key, 6), axis_at), (blocks,), jnp.float32, low / len(shards), largest / len(shards))
        return jnp.repeat(jnp.exp(draws), shape[axis_at] // blocks).reshape((-1,) + (1,) * (len(shape) - axis_at - 1))

    loudness = one(*shards[0])
    for cut in shards[1:]:
        loudness = loudness * one(*cut)
    return loudness


def normal_values(own_key, extent, spread, most, shards=(), dtype=jnp.bfloat16):
    factor_of = block_levels(own_key, extent, shards, -0.22, 0.18) if shards else 1.0
    values = jax.random.normal(own_key, extent, jnp.float32) * spread * factor_of
    return jnp.minimum(jnp.maximum(values, -most), most).astype(dtype)


def setup_inputs(seed: int = 0) -> dict:
    seeds = jax.random.split(jax.random.key(seed), 5)
    three_centre = normal_values(seeds[0], (NAUX, NORB, NORB), NORB ** -0.5, 0.125, ((0, 48), (1, 16)))
    screening = with_ends((jax.random.randint(seeds[1], (NAUX, NOB, NOB), 0, 4) < 3).astype(jnp.int32), jax.random.fold_in(seeds[1], 1), 0, 1)
    coefficients = normal_values(seeds[2], (NORB, NOCC), (NAUX * NOCC) ** -0.5, 0.015625)
    occ_pattern = with_ends((jax.random.randint(seeds[3], (NOB, OCC_BLOCKS), 0, 4) < 3).astype(jnp.int32), jax.random.fold_in(seeds[3], 1), 0, 1)
    return {"three_centre": three_centre, "screening": screening, "coefficients": coefficients, "occ_pattern": occ_pattern}


def reference(three_centre, screening, coefficients, occ_pattern):
    occ_mask = occ_pattern.astype(jnp.bfloat16)
    masked_c = (coefficients.reshape(NOB, OBS, OCC_BLOCKS, OCC_DEV) * occ_mask[:, None, :, None]).reshape(NORB, NOCC)

    def accumulate(running, inputs):
        slab, screen_rows = inputs
        masked = (slab.reshape(NOB, OBS, NOB, OBS) * screen_rows.astype(jnp.bfloat16)[:, None, :, None]).reshape(NORB, NORB)
        halved = jnp.dot(masked, masked_c, preferred_element_type=jnp.float32).astype(jnp.bfloat16)
        return running + jnp.dot(halved, halved.T, preferred_element_type=jnp.float32), None

    initial = jnp.zeros((NORB, NORB), jnp.float32)
    result, unused = lax.scan(accumulate, initial, (three_centre, screening))
    return result
```

```python
import jax
import jax.numpy as jnp
from jax import lax
from jax.experimental import pallas as pl
from jax.experimental.pallas import tpu as pltpu
from jax.sharding import PartitionSpec as P

MESH = pl.DeviceIdType.MESH
X, Y, Z = 4, 8, 12
BLK = 128
NT = (((1,), (1,)), ((), ()))


def kernel(t_hbm, scr_ref, c_hbm, occ_ref, out_ref,
           tv, cv, h, ring, blk, swp, xr, xs, zr, zt, ze, zf, full,
           load_sem, part_s, part_r, ring_s, ring_r, swp_s, swp_r,
           xs_s, xs_r, zs_s, zs_r, e_s, e_r, zg_s, zg_r, xg_s, xg_r):
    aux = lax.axis_index("aux")
    orb = lax.axis_index("orb")
    x, z = aux // Z, aux % Z
    y, core = orb // 2, orb % 2
    other = 1 - core
    high = y // 4
    sg, kk, hh = z // 4, (z // 2) % 2, z % 2
    nocc = cv.shape[1]

    def dev(xx, zz, yy, cc):
        return (xx * Z + zz, yy * 2 + cc)

    def remote(src, dst, s_sem, r_sem, where):
        return pltpu.make_async_remote_copy(
            src_ref=src, dst_ref=dst, send_sem=s_sem, recv_sem=r_sem,
            device_id=where, device_id_type=MESH)

    partner = dev(x, z, y, other)
    nexts = (dev(x, z, (y + Y - 1) % Y, core), dev(x, z, (y + 1) % Y, core))

    def mirror(g):
        s = g + 1
        dy = ((sg - 1) * (sg - 2) // 2) * s + sg * (2 - sg) * (Y - s) + (sg * (sg - 1) // 2) * 4
        flip = ((sg - 1) * (sg - 2) // 2) + (sg * (sg - 1) // 2) * 2
        return dev(x, 4 * flip + 2 * core + hh, (y + dy) % Y, kk)

    def x_peer(d):
        return dev((x + d) % X, z, y, core)

    def z_peer(d):
        return dev(x, (z + d) % Z, y, core)

    def load_t(p):
        return pltpu.make_async_copy(t_hbm.at[p], tv.at[p], load_sem.at[p])

    crows = cv.shape[0] // 4

    def load_c(q):
        rows = pl.ds(q * crows, crows)
        return pltpu.make_async_copy(c_hbm.at[rows], cv.at[rows], load_sem.at[4 + q])

    for q in range(4):
        load_c(q).start()
    for p in range(4):
        load_t(p).start()

    barrier = pltpu.get_barrier_semaphore()

    def signal(where):
        pl.semaphore_signal(barrier, inc=1, device_id=where, device_id_type=MESH)

    signal(partner)
    signal(nexts[0])
    signal(nexts[1])
    for d in range(1, X):
        signal(x_peer(d))

    @pl.loop(1, Z)
    def _(d):
        signal(z_peer(d))

    signal(mirror(2))

    @pl.when(z < 8)
    def _():
        signal(mirror(0))
        signal(mirror(1))

    occ = occ_ref[...].astype(jnp.float32).astype(jnp.bfloat16)
    nslices = occ.shape[1]
    spread = (lax.broadcasted_iota(jnp.int32, (nslices, nocc), 1) // (nocc // nslices)
              == lax.broadcasted_iota(jnp.int32, (nslices, nocc), 0)).astype(jnp.float32).astype(jnp.bfloat16)
    occ_mask = jnp.dot(occ, spread, preferred_element_type=jnp.float32).astype(jnp.bfloat16)
    screen = scr_ref[...].reshape(4, 16).astype(jnp.float32).astype(jnp.bfloat16)
    widen = (lax.broadcasted_iota(jnp.int32, (16, 2048), 1) // BLK
             == lax.broadcasted_iota(jnp.int32, (16, 2048), 0)).astype(jnp.float32).astype(jnp.bfloat16)
    scr_mask = jnp.dot(screen, widen, preferred_element_type=jnp.float32).astype(jnp.bfloat16)

    for q in range(4):
        load_c(q).wait()
        for nb in range(4 * q, 4 * q + 4):
            rows = slice(nb * BLK, (nb + 1) * BLK)
            cv[rows, :] = cv[rows, :] * occ_mask[nb:nb + 1, :]

    for p in range(4):
        load_t(p).wait()
        tv[p] = tv[p] * scr_mask[p:p + 1, :]

    pl.semaphore_wait(barrier, 20 - 2 * (z // 8))

    def hop(d, slot):
        if slot < 2:
            src = h.at[core, slot, d]
        elif slot < 6:
            src = ring.at[d, slot - 2]
        else:
            target = (y + Y - 1) % Y if d == 0 else (y + 1) % Y
            src = ring.at[d, 4 + target // 4]
        return remote(src, ring.at[d, slot], ring_s.at[d, slot], ring_r.at[d, slot], nexts[d])

    def to_partner(t, d):
        return remote(h.at[core, t, d], h.at[core, t, d], part_s.at[t, d], part_r.at[t, d], partner)

    for t in range(2):
        lhs = tv[2 * t:2 * t + 2].reshape(2 * BLK, tv.shape[2])
        for n in range(nocc // 256):
            cols = slice(n * 256, (n + 1) * 256)
            r = jnp.dot(lhs, cv[:, cols], preferred_element_type=jnp.float32).astype(jnp.bfloat16)
            h[core, t, 0, :, cols] = r[:BLK]
            h[core, t, 1, :, cols] = r[BLK:]
        for d in range(2):
            hop(d, t).start()
        for d in range(2):
            to_partner(t, d).start()

    def dot_nt(a, b):
        return lax.dot_general(a, b, NT, preferred_element_type=jnp.float32)

    for t in range(2):
        for d in range(2):
            to_partner(t, d).wait_recv()
    for who, put in ((core, "own"), (other, "swap")):
        total = None
        for t in range(2):
            for d in range(2):
                v = dot_nt(h[who, t, d], h[core, t, d])
                total = v if total is None else total + v
        if put == "own":
            blk[0, core, 2] = total
        else:
            swp[0, 2] = total
    blk[1, core, 2] = jnp.zeros((BLK, BLK), jnp.float32)
    swp[1, 2] = jnp.zeros((BLK, BLK), jnp.float32)

    def pair(who, t, d, slot, rows_own):
        a, b = h[who, t, d], ring[d, slot]
        return dot_nt(a, b) if rows_own else dot_nt(b, a)

    def ring_step(s, t):
        slot = 2 * (s - 1) + t
        for d in range(2):
            hop(d, slot).wait_recv()
            if slot < 4:
                hop(d, slot + 2).start()
            elif slot == 5:
                hop(d, 6).start()
        for d in range(2):
            own = pair(core, t, d, slot, d == 0)
            away = pair(other, t, d, slot, d == 0)
            if t == 0:
                blk[s - 1, core, d] = own
                swp[s - 1, d] = away
            else:
                blk[s - 1, core, d] += own
                swp[s - 1, d] += away

    def antipode():
        for d in range(2):
            hop(d, 6).wait_recv()

        for side in range(2):
            @pl.when(high == side)
            def _():
                blk[2, core, 2] = pair(core, side, 0, 6, side == 0) + pair(core, side, 1, 6, side == 0)
                swp[2, 2] = pair(other, side, 0, 6, side == 0) + pair(other, side, 1, 6, side == 0)

    def swap(g):
        return remote(swp.at[g], blk.at[g, core], swp_s.at[g], swp_r.at[g], partner)

    def wait_bytes(ref, sem):
        pltpu.make_async_copy(ref, ref, sem).wait()

    def swap_start(g):
        swap(g).start()

    def xrs_start(g):
        swap(g).wait_recv()
        for d in range(1, X):
            xx = (x + d) % X
            remote(blk.at[g, :, :, pl.ds(pl.multiple_of(xx * 32, 32), 32), :], xr.at[g, d - 1],
                   xs_s.at[g], xs_r.at[g], x_peer(d)).start()

    def zrs_start(g):
        wait_bytes(xr.at[g], xs_r.at[g])
        mine = blk[g, :, :, pl.ds(pl.multiple_of(x * 32, 32), 32), :]
        xs[g] = (mine + xr[g, 0]) + (xr[g, 1] + xr[g, 2])

        @pl.loop(1, Z)
        def _(d):
            zz = (z + d) % Z
            remote(xs.at[g, (zz // 2) % 2, zz // 4, pl.ds(pl.multiple_of((zz % 2) * 16, 16), 16), :],
                   zr.at[g, d - 1], zs_s.at[g], zs_r.at[g], z_peer(d)).start()

    def exchange(g):
        return remote(zt.at[g], ze.at[g], e_s.at[g], e_r.at[g], mirror(g))

    def when_mirrored(g, fn):
        if g == 2:
            fn()
        else:
            pl.when(z < 8)(fn)

    def ex_start(g):
        wait_bytes(zr.at[g], zs_r.at[g])
        total = xs[g, kk, sg, pl.ds(pl.multiple_of(hh * 16, 16), 16), :]
        for d in range(Z - 1):
            total = total + zr[g, d]
        zt[g] = total
        when_mirrored(g, lambda: exchange(g).start())

    def my_tile(g):
        return full.at[g, kk, sg, pl.ds(pl.multiple_of(x * 32 + hh * 16, 16), 16), :]

    def zag_start(g):
        def add():
            exchange(g).wait_recv()
            zf[g] = zt[g] + ze[g]

        when_mirrored(g, add)
        if g != 2:
            @pl.when(z >= 8)
            def _():
                zf[g] = zt[g]
        my_tile(g)[...] = zf[g]

        @pl.loop(1, Z)
        def _(d):
            remote(zf.at[g], my_tile(g), zg_s.at[g], zg_r.at[g], z_peer(d)).start()

    def x_slab(g):
        return full.at[g, :, :, pl.ds(pl.multiple_of(x * 32, 32), 32), :]

    def xag_start(g):
        wait_bytes(zr.at[g], zg_r.at[g])
        for d in range(1, X):
            remote(x_slab(g), x_slab(g), xg_s.at[g], xg_r.at[g], x_peer(d)).start()

    def put(d, k, value):
        out_ref[:, pl.ds(pl.multiple_of((2 * d + k) * BLK, BLK), BLK)] = value

    def finish(g):
        wait_bytes(xr.at[g], xg_r.at[g])
        s = g + 1
        for k in range(2):
            put((y + s) % Y, k, full[g, k, 0])
            put((y + Y - s) % Y, k, full[g, k, 1].T)
            if g == 0:
                put(y, k, full[g, k, 2])
        if g == 2:
            for side in range(2):
                @pl.when(high == side)
                def _():
                    for k in range(2):
                        v = full[g, k, 2]
                        put((y + 4) % Y, k, v if side == 0 else v.T)

    ring_step(1, 0)
    ring_step(1, 1)
    swap_start(0)
    ring_step(2, 0)
    xrs_start(0)
    ring_step(2, 1)
    swap_start(1)
    zrs_start(0)
    ring_step(3, 0)
    ex_start(0)
    xrs_start(1)
    ring_step(3, 1)
    zag_start(0)
    zrs_start(1)
    antipode()
    swap_start(2)
    xag_start(0)
    xrs_start(2)
    ex_start(1)
    zag_start(1)
    zrs_start(2)
    finish(0)
    xag_start(1)
    ex_start(2)
    zag_start(2)
    finish(1)
    xag_start(2)
    finish(2)

    for t in range(2):
        for d in range(2):
            to_partner(t, d).wait_send()
    for d in range(2):
        for slot in range(7):
            hop(d, slot).wait_send()
    for g in range(3):
        swap(g).wait_send()
        wait_bytes(xr.at[g], xs_s.at[g])
        wait_bytes(zr.at[g], zs_s.at[g])
        when_mirrored(g, lambda: exchange(g).wait_send())
        wait_bytes(zr.at[g], zg_s.at[g])
        wait_bytes(xr.at[g], xg_s.at[g])


def on_device(three_centre, screening, coefficients, occ_pattern):
    nocc = coefficients.shape[1]
    norb = coefficients.shape[0]
    bf, f32 = jnp.bfloat16, jnp.float32
    dma = pltpu.SemaphoreType.DMA
    vmem = pltpu.VMEM
    return pl.pallas_call(
        kernel,
        out_shape=jax.ShapeDtypeStruct((BLK, norb), f32),
        in_specs=[
            pl.BlockSpec(memory_space=pl.ANY),
            pl.BlockSpec(memory_space=vmem),
            pl.BlockSpec(memory_space=pl.ANY),
            pl.BlockSpec(memory_space=vmem),
        ],
        out_specs=pl.BlockSpec(memory_space=vmem),
        scratch_shapes=[
            vmem((4, BLK, norb), bf),
            vmem((norb, nocc), bf),
            vmem((2, 2, 2, BLK, nocc), bf),
            vmem((2, 7, BLK, nocc), bf),
            vmem((3, 2, 3, BLK, BLK), f32),
            vmem((3, 3, BLK, BLK), f32),
            vmem((3, X - 1, 2, 3, 32, BLK), f32),
            vmem((3, 2, 3, 32, BLK), f32),
            vmem((3, Z - 1, 16, BLK), f32),
            vmem((3, 16, BLK), f32),
            vmem((3, 16, BLK), f32),
            vmem((3, 16, BLK), f32),
            vmem((3, 2, 3, BLK, BLK), f32),
            dma((8,)),
            dma((2, 2)), dma((2, 2)),
            dma((2, 7)), dma((2, 7)),
            dma((3,)), dma((3,)),
            dma((3,)), dma((3,)),
            dma((3,)), dma((3,)),
            dma((3,)), dma((3,)),
            dma((3,)), dma((3,)),
            dma((3,)), dma((3,)),
        ],
        compiler_params=pltpu.CompilerParams(
            collective_id=0, has_side_effects=True, vmem_limit_bytes=48 * 2**20),
        cost_estimate=pl.CostEstimate(flops=3 * 10**9, bytes_accessed=6 * 10**6, transcendentals=0),
    )(three_centre, screening, coefficients, occ_pattern)


def solution(mesh):
    return jax.shard_map(
        on_device,
        mesh=mesh,
        in_specs=(P("aux", "orb", None), P("aux", "orb", None), P(), P()),
        out_specs=P("orb", None),
        check_vma=False,
    )
```

```python
import jax
import jax.numpy as jnp
from jax import lax
from jax.experimental import pallas as pl
from jax.experimental.pallas import tpu as pltpu
from jax.sharding import PartitionSpec as P

MESH = pl.DeviceIdType.MESH
X, Y, Z = 4, 8, 12
BLK = 128
NT = (((1,), (1,)), ((), ()))


SIGNS = (3, 2, 2, 1)
TILE = (16, 16, 16, 8)
OWNERS = (12, 8, 8, 8)
GROUPS = len(SIGNS)
QUART = BLK // X


def kernel(t_hbm, scr_hbm, c_hbm, occ_hbm, out_ref,
           tv, cv, scr_ref, occ_ref, h, ring,
           blk0, blk1, blk2, blk3, far0, far1, far2, far3,
           xa0, xa1, xa2, xa3, xb0, xb1, xb2, xb3, xs0, xs1, xs2, xs3,
           zr0, zr1, zr2, zr3, zt0, zt1, zt2, zt3, ze0, ze1, ze2, ze3,
           full0, full1, full2, full3,
           load_sem, part_s, part_r, ring_s, ring_r,
           xs_s, xs_r, xt_s, xt_r, zs_s, zs_r, e_s, e_r, zg_s, zg_r, xg_s, xg_r):
    blk, far = (blk0, blk1, blk2, blk3), (far0, far1, far2, far3)
    xa, xb, xs = (xa0, xa1, xa2, xa3), (xb0, xb1, xb2, xb3), (xs0, xs1, xs2, xs3)
    zr, zt, ze = (zr0, zr1, zr2, zr3), (zt0, zt1, zt2, zt3), (ze0, ze1, ze2, ze3)
    full = (full0, full1, full2, full3)
    aux = lax.axis_index("aux")
    orb = lax.axis_index("orb")
    x, z = aux // Z, aux % Z
    y, core = orb // 2, orb % 2
    other = 1 - core
    high = y // 4
    nocc = cv.shape[1]

    def dev(xx, zz, yy, cc):
        return (xx * Z + zz, yy * 2 + cc)

    def remote(src, dst, s_sem, r_sem, where):
        return pltpu.make_async_remote_copy(
            src_ref=src, dst_ref=dst, send_sem=s_sem, recv_sem=r_sem,
            device_id=where, device_id_type=MESH)

    partner = dev(x, z, y, other)
    nexts = (dev(x, z, (y + Y - 1) % Y, core), dev(x, z, (y + 1) % Y, core))

    def tile_of(g, zz):
        if g == 3:
            return 0, (zz // 4 + core) % 2, (zz % 4) * TILE[g]
        a, b, part = zz // 4, (zz // 2) % 2, zz % 2
        flip = (a + (y // 2 if g == 1 else y)) % 2
        sign = (1 - a // 2) * flip + (a // 2) * 2 if g == 0 else flip
        return sign, (b + core) % 2, part * TILE[g]

    def mirror(g):
        sign, k, _ = tile_of(g, z)
        dy = 4 if g == 3 else (1 - sign) * (g + 1) + sign * (Y - g - 1)
        return dev(x, z, (y + dy) % Y, k)

    def x_peer(d, cc):
        return dev((x + d) % X, z, y, cc)

    def z_peer(d):
        return dev(x, (z + d) % Z, y, core)

    def load_t(p):
        return pltpu.make_async_copy(t_hbm.at[p], tv.at[p], load_sem.at[p])

    crows = cv.shape[0] // 4

    def load_c(q):
        rows = pl.ds(q * crows, crows)
        return pltpu.make_async_copy(c_hbm.at[rows], cv.at[rows], load_sem.at[4 + q])

    load_occ = pltpu.make_async_copy(occ_hbm, occ_ref, load_sem.at[8])
    load_scr = pltpu.make_async_copy(scr_hbm, scr_ref, load_sem.at[9])
    load_occ.start()
    load_scr.start()
    for q in range(4):
        load_c(q).start()
    for p in range(4):
        load_t(p).start()

    barrier = pltpu.get_barrier_semaphore()

    def signal(where):
        pl.semaphore_signal(barrier, inc=1, device_id=where, device_id_type=MESH)

    signal(partner)
    signal(nexts[0])
    signal(nexts[1])
    for d in range(X):
        if d:
            signal(x_peer(d, core))
            signal(x_peer(d, other))

    @pl.loop(1, Z)
    def _(d):
        signal(z_peer(d))

    @pl.when(z < 8)
    def _():
        for g in range(GROUPS):
            signal(mirror(g))

    load_occ.wait()
    load_scr.wait()
    occ = occ_ref[...].astype(jnp.float32).astype(jnp.bfloat16)
    nslices = occ.shape[1]
    spread = (lax.broadcasted_iota(jnp.int32, (nslices, nocc), 1) // (nocc // nslices)
              == lax.broadcasted_iota(jnp.int32, (nslices, nocc), 0)).astype(jnp.float32).astype(jnp.bfloat16)
    occ_mask = jnp.dot(occ, spread, preferred_element_type=jnp.float32).astype(jnp.bfloat16)
    screen = scr_ref[...].reshape(4, 16).astype(jnp.float32).astype(jnp.bfloat16)
    widen = (lax.broadcasted_iota(jnp.int32, (16, 2048), 1) // BLK
             == lax.broadcasted_iota(jnp.int32, (16, 2048), 0)).astype(jnp.float32).astype(jnp.bfloat16)
    scr_mask = jnp.dot(screen, widen, preferred_element_type=jnp.float32).astype(jnp.bfloat16)

    for q in range(4):
        load_c(q).wait()
        for nb in range(4 * q, 4 * q + 4):
            rows = slice(nb * BLK, (nb + 1) * BLK)
            cv[rows, :] = cv[rows, :] * occ_mask[nb:nb + 1, :]

    for p in range(4):
        load_t(p).wait()
        tv[p] = tv[p] * scr_mask[p:p + 1, :]

    pl.semaphore_wait(barrier, 24 - 4 * (z // 8))

    def hop(d, slot):
        if slot < 2:
            src = h.at[core, slot, d]
        elif slot < 6:
            src = ring.at[d, slot - 2]
        else:
            target = (y + Y - 1) % Y if d == 0 else (y + 1) % Y
            src = ring.at[d, 4 + target // 4]
        return remote(src, ring.at[d, slot], ring_s.at[d, slot], ring_r.at[d, slot], nexts[d])

    def to_partner(t, d):
        return remote(h.at[core, t, d], h.at[core, t, d], part_s.at[t, d], part_r.at[t, d], partner)

    for t in range(2):
        lhs = tv[2 * t:2 * t + 2].reshape(2 * BLK, tv.shape[2])
        for n in range(nocc // 256):
            cols = slice(n * 256, (n + 1) * 256)
            r = jnp.dot(lhs, cv[:, cols], preferred_element_type=jnp.float32).astype(jnp.bfloat16)
            h[core, t, 0, :, cols] = r[:BLK]
            h[core, t, 1, :, cols] = r[BLK:]
        for d in range(2):
            hop(d, t).start()
        for d in range(2):
            to_partner(t, d).start()

    def dot_nt(a, b):
        return lax.dot_general(a, b, NT, preferred_element_type=jnp.float32)

    for t in range(2):
        for d in range(2):
            to_partner(t, d).wait_recv()
    for who, put in ((core, blk0), (other, far0)):
        total = None
        for t in range(2):
            for d in range(2):
                v = dot_nt(h[who, t, d], h[core, t, d])
                total = v if total is None else total + v
        put[2] = total

    def pair(who, t, d, slot, rows_own):
        a, b = h[who, t, d], ring[d, slot]
        return dot_nt(a, b) if rows_own else dot_nt(b, a)

    def ring_step(s, t):
        slot = 2 * (s - 1) + t
        for d in range(2):
            hop(d, slot).wait_recv()
            if slot < 4:
                hop(d, slot + 2).start()
            elif slot == 5:
                hop(d, 6).start()
        for d in range(2):
            own = pair(core, t, d, slot, d == 0)
            away = pair(other, t, d, slot, d == 0)
            if t == 0:
                blk[s - 1][d] = own
                far[s - 1][d] = away
            else:
                blk[s - 1][d] += own
                far[s - 1][d] += away

    def antipode():
        for d in range(2):
            hop(d, 6).wait_recv()

        for side in range(2):
            @pl.when(high == side)
            def _():
                blk[3][0] = pair(core, side, 0, 6, side == 0) + pair(core, side, 1, 6, side == 0)
                far[3][0] = pair(other, side, 0, 6, side == 0) + pair(other, side, 1, 6, side == 0)

    def wait_bytes(ref, sem):
        pltpu.make_async_copy(ref, ref, sem).wait()

    def quarter(xx):
        return pl.ds(pl.multiple_of(xx * QUART, QUART), QUART)

    def when_owner(g, fn):
        if OWNERS[g] == Z:
            fn()
        else:
            pl.when(z < OWNERS[g])(fn)

    def when_mirrored(fn):
        pl.when(z < 8)(fn)

    def xrs_start(g):
        for d in range(X):
            q = quarter((x + d) % X)
            if d:
                remote(blk[g].at[:, q, :], xa[g].at[d - 1], xs_s.at[g], xs_r.at[g], x_peer(d, core)).start()
            remote(far[g].at[:, q, :], xb[g].at[d], xt_s.at[g], xt_r.at[g], x_peer(d, other)).start()

    def tile(ref, g, zz, first=0):
        sign, k, row = tile_of(g, zz)
        return ref.at[k, sign, pl.ds(pl.multiple_of(first + row, TILE[g]), TILE[g]), :]

    def zrs_start(g):
        wait_bytes(xa[g], xs_r.at[g])
        wait_bytes(xb[g], xt_r.at[g])
        xs[g][core] = (blk[g][:, quarter(x), :] + xa[g][0]) + (xa[g][1] + xa[g][2])
        xs[g][other] = (xb[g][0] + xb[g][1]) + (xb[g][2] + xb[g][3])

        @pl.loop(1, Z)
        def _(d):
            zz = (z + d) % Z

            def send():
                remote(tile(xs[g], g, zz), zr[g].at[d - 1], zs_s.at[g], zs_r.at[g], z_peer(d)).start()

            if OWNERS[g] == Z:
                send()
            else:
                pl.when(zz < OWNERS[g])(send)

    def exchange(g):
        return remote(zt[g], ze[g], e_s.at[g], e_r.at[g], mirror(g))

    def ex_start(g):
        def collect():
            wait_bytes(zr[g], zs_r.at[g])
            total = tile(xs[g], g, z)[...]
            for d in range(Z - 1):
                total = total + zr[g][d]
            zt[g][...] = total

        when_owner(g, collect)
        when_mirrored(lambda: exchange(g).start())

    def zag_start(g):
        @pl.when(z < 8)
        def _():
            exchange(g).wait_recv()
            tile(full[g], g, z, x * QUART)[...] = zt[g][...] + ze[g][...]

        if g == 0:
            @pl.when(z >= 8)
            def _():
                tile(full[g], g, z, x * QUART)[...] = zt[g][...]

        def spread_out():
            @pl.loop(1, Z)
            def _(d):
                mine = tile(full[g], g, z, x * QUART)
                remote(mine, mine, zg_s.at[g], zg_r.at[g], z_peer(d)).start()

        when_owner(g, spread_out)

    def x_slab(g):
        return full[g].at[:, :, quarter(x), :]

    def three_quarters(g):
        return full[g].at[:, :, pl.ds(0, 3 * QUART), :]

    def xag_start(g):
        if OWNERS[g] == Z:
            wait_bytes(zr[g], zg_r.at[g])
        else:
            @pl.when(z < OWNERS[g])
            def _():
                wait_bytes(zr[g].at[pl.ds(0, OWNERS[g] - 1)], zg_r.at[g])

            @pl.when(z >= OWNERS[g])
            def _():
                wait_bytes(zr[g].at[pl.ds(0, OWNERS[g])], zg_r.at[g])
        for d in range(1, X):
            remote(x_slab(g), x_slab(g), xg_s.at[g], xg_r.at[g], x_peer(d, core)).start()

    def put(d, k, value):
        out_ref[:, pl.ds(pl.multiple_of((2 * d + k) * BLK, BLK), BLK)] = value

    def finish(g):
        wait_bytes(three_quarters(g), xg_r.at[g])
        s = g + 1
        if g < 3:
            for k in range(2):
                put((y + s) % Y, k, full[g][k, 0])
                put((y + Y - s) % Y, k, full[g][k, 1].T)
                if g == 0:
                    put(y, k, full[g][k, 2])
        else:
            for side in range(2):
                @pl.when(high == side)
                def _():
                    for k in range(2):
                        v = full[g][k, 0]
                        put((y + 4) % Y, k, v if side == 0 else v.T)

    ring_step(1, 0)
    ring_step(1, 1)
    xrs_start(0)
    ring_step(2, 0)
    ring_step(2, 1)
    xrs_start(1)
    zrs_start(0)
    ring_step(3, 0)
    ring_step(3, 1)
    xrs_start(2)
    ex_start(0)
    zrs_start(1)
    antipode()
    xrs_start(3)
    zag_start(0)
    ex_start(1)
    zrs_start(2)
    zrs_start(3)
    xag_start(0)
    zag_start(1)
    ex_start(2)
    ex_start(3)
    xag_start(1)
    finish(0)
    zag_start(2)
    zag_start(3)
    finish(1)
    xag_start(2)
    xag_start(3)
    finish(2)
    finish(3)

    for t in range(2):
        for d in range(2):
            to_partner(t, d).wait_send()
    for d in range(2):
        for slot in range(7):
            hop(d, slot).wait_send()
    for g in range(GROUPS):
        wait_bytes(xa[g], xs_s.at[g])
        wait_bytes(xb[g], xt_s.at[g])
        if OWNERS[g] == Z:
            wait_bytes(zr[g], zs_s.at[g])
            wait_bytes(zr[g], zg_s.at[g])
        else:
            @pl.when(z < OWNERS[g])
            def _():
                wait_bytes(zr[g].at[pl.ds(0, OWNERS[g] - 1)], zs_s.at[g])
                wait_bytes(zr[g], zg_s.at[g])

            @pl.when(z >= OWNERS[g])
            def _():
                wait_bytes(zr[g].at[pl.ds(0, OWNERS[g])], zs_s.at[g])
        when_mirrored(lambda: exchange(g).wait_send())
        wait_bytes(three_quarters(g), xg_s.at[g])


def on_device(three_centre, screening, coefficients, occ_pattern):
    nocc = coefficients.shape[1]
    norb = coefficients.shape[0]
    bf, f32 = jnp.bfloat16, jnp.float32
    dma = pltpu.SemaphoreType.DMA
    vmem = pltpu.VMEM
    return pl.pallas_call(
        kernel,
        out_shape=jax.ShapeDtypeStruct((BLK, norb), f32),
        in_specs=[pl.BlockSpec(memory_space=pl.ANY)] * 4,
        out_specs=pl.BlockSpec(memory_space=vmem),
        scratch_shapes=[
            vmem((4, BLK, norb), bf),
            vmem((norb, nocc), bf),
            vmem(screening.shape, jnp.int32),
            vmem(occ_pattern.shape, jnp.int32),
            vmem((2, 2, 2, BLK, nocc), bf),
            vmem((2, 7, BLK, nocc), bf),
            *[vmem((n, BLK, BLK), f32) for n in SIGNS],
            *[vmem((n, BLK, BLK), f32) for n in SIGNS],
            *[vmem((X - 1, n, QUART, BLK), f32) for n in SIGNS],
            *[vmem((X, n, QUART, BLK), f32) for n in SIGNS],
            *[vmem((2, n, QUART, BLK), f32) for n in SIGNS],
            *[vmem((Z - 1, r, BLK), f32) for r in TILE],
            *[vmem((r, BLK), f32) for r in TILE],
            *[vmem((r, BLK), f32) for r in TILE],
            *[vmem((2, n, BLK, BLK), f32) for n in SIGNS],
            dma((10,)),
            dma((2, 2)), dma((2, 2)),
            dma((2, 7)), dma((2, 7)),
            *[dma((GROUPS,))] * 12,
        ],
        compiler_params=pltpu.CompilerParams(
            collective_id=0, has_side_effects=True, vmem_limit_bytes=60 * 2**20),
        cost_estimate=pl.CostEstimate(flops=3 * 10**9, bytes_accessed=6 * 10**6, transcendentals=0),
    )(three_centre, screening, coefficients, occ_pattern)


def solution(mesh):
    return jax.shard_map(
        on_device,
        mesh=mesh,
        in_specs=(P("aux", "orb", None), P("aux", "orb", None), P(), P()),
        out_specs=P("orb", None),
        check_vma=False,
    )
```

```python
import jax
import jax.numpy as jnp
from jax import lax
from jax.experimental import pallas as pl
from jax.experimental.pallas import tpu as pltpu
from jax.sharding import PartitionSpec as P

MESH = pl.DeviceIdType.MESH
X, Y, Z = 4, 8, 12
BLK = 128
NT = (((1,), (1,)), ((), ()))


SIGNS = (3, 2, 2, 1)
TILE = (16, 16, 16, 8)
OWNERS = (12, 8, 8, 8)
GROUPS = len(SIGNS)
QUART = BLK // X


def kernel(t_hbm, scr_hbm, c_hbm, occ_hbm, out_ref,
           tv, cv, scr_ref, occ_ref, h, ring,
           blk0, blk1, blk2, blk3, far0, far1, far2, far3,
           xa0, xa1, xa2, xa3, xb0, xb1, xb2, xb3, xs0, xs1, xs2, xs3,
           zr0, zr1, zr2, zr3, zt0, zt1, zt2, zt3, ze0, ze1, ze2, ze3,
           full0, full1, full2, full3,
           load_sem, part_s, part_r, ring_s, ring_r,
           xs_s, xs_r, xt_s, xt_r, zs_s, zs_r, e_s, e_r, zg_s, zg_r, xg_s, xh_s, xg_r):
    blk, far = (blk0, blk1, blk2, blk3), (far0, far1, far2, far3)
    xa, xb, xs = (xa0, xa1, xa2, xa3), (xb0, xb1, xb2, xb3), (xs0, xs1, xs2, xs3)
    zr, zt, ze = (zr0, zr1, zr2, zr3), (zt0, zt1, zt2, zt3), (ze0, ze1, ze2, ze3)
    full = (full0, full1, full2, full3)
    aux = lax.axis_index("aux")
    orb = lax.axis_index("orb")
    x, z = aux // Z, aux % Z
    y, core = orb // 2, orb % 2
    other = 1 - core
    high = y // 4
    nocc = cv.shape[1]

    def dev(xx, zz, yy, cc):
        return (xx * Z + zz, yy * 2 + cc)

    def remote(src, dst, s_sem, r_sem, where):
        return pltpu.make_async_remote_copy(
            src_ref=src, dst_ref=dst, send_sem=s_sem, recv_sem=r_sem,
            device_id=where, device_id_type=MESH)

    partner = dev(x, z, y, other)
    nexts = (dev(x, z, (y + Y - 1) % Y, core), dev(x, z, (y + 1) % Y, core))

    def tile_of(g, zz):
        if g == 3:
            return 0, (zz // 4 + core) % 2, (zz % 4) * TILE[g]
        a, b, part = zz // 4, (zz // 2) % 2, zz % 2
        flip = (a + (y // 2 if g == 1 else y)) % 2
        sign = (1 - a // 2) * flip + (a // 2) * 2 if g == 0 else flip
        return sign, (b + core) % 2, part * TILE[g]

    def mirror(g):
        sign, k, _ = tile_of(g, z)
        dy = 4 if g == 3 else (1 - sign) * (g + 1) + sign * (Y - g - 1)
        return dev(x, z, (y + dy) % Y, k)

    def x_peer(d, cc):
        return dev((x + d) % X, z, y, cc)

    def z_peer(d):
        return dev(x, (z + d) % Z, y, core)

    def load_t(p):
        return pltpu.make_async_copy(t_hbm.at[p], tv.at[p], load_sem.at[p])

    crows = cv.shape[0] // 4

    def load_c(q):
        rows = pl.ds(q * crows, crows)
        return pltpu.make_async_copy(c_hbm.at[rows], cv.at[rows], load_sem.at[4 + q])

    load_occ = pltpu.make_async_copy(occ_hbm, occ_ref, load_sem.at[8])
    load_scr = pltpu.make_async_copy(scr_hbm, scr_ref, load_sem.at[9])
    load_occ.start()
    load_scr.start()
    for q in range(4):
        load_c(q).start()
    for p in range(4):
        load_t(p).start()

    barrier = pltpu.get_barrier_semaphore()

    def signal(where):
        pl.semaphore_signal(barrier, inc=1, device_id=where, device_id_type=MESH)

    signal(partner)
    signal(nexts[0])
    signal(nexts[1])
    for d in range(X):
        if d:
            signal(x_peer(d, core))
            signal(x_peer(d, other))

    @pl.loop(1, Z)
    def _(d):
        signal(z_peer(d))

    @pl.when(z < 8)
    def _():
        for g in range(GROUPS):
            signal(mirror(g))

    load_occ.wait()
    load_scr.wait()
    occ = occ_ref[...].astype(jnp.float32).astype(jnp.bfloat16)
    nslices = occ.shape[1]
    spread = (lax.broadcasted_iota(jnp.int32, (nslices, nocc), 1) // (nocc // nslices)
              == lax.broadcasted_iota(jnp.int32, (nslices, nocc), 0)).astype(jnp.float32).astype(jnp.bfloat16)
    occ_mask = jnp.dot(occ, spread, preferred_element_type=jnp.float32).astype(jnp.bfloat16)
    screen = scr_ref[...].reshape(4, 16).astype(jnp.float32).astype(jnp.bfloat16)
    widen = (lax.broadcasted_iota(jnp.int32, (16, 2048), 1) // BLK
             == lax.broadcasted_iota(jnp.int32, (16, 2048), 0)).astype(jnp.float32).astype(jnp.bfloat16)
    scr_mask = jnp.dot(screen, widen, preferred_element_type=jnp.float32).astype(jnp.bfloat16)

    for q in range(4):
        load_c(q).wait()
        for nb in range(4 * q, 4 * q + 4):
            rows = slice(nb * BLK, (nb + 1) * BLK)
            cv[rows, :] = cv[rows, :] * occ_mask[nb:nb + 1, :]

    def hop(d, slot):
        if slot < 2:
            src = h.at[core, slot, d]
        elif slot < 6:
            src = ring.at[d, slot - 2]
        else:
            target = (y + Y - 1) % Y if d == 0 else (y + 1) % Y
            src = ring.at[d, 4 + target // 4]
        return remote(src, ring.at[d, slot], ring_s.at[d, slot], ring_r.at[d, slot], nexts[d])

    def to_partner(t, d):
        return remote(h.at[core, t, d], h.at[core, t, d], part_s.at[t, d], part_r.at[t, d], partner)

    for t in range(2):
        for p in (2 * t, 2 * t + 1):
            load_t(p).wait()
            tv[p] = tv[p] * scr_mask[p:p + 1, :]
        lhs = tv[2 * t:2 * t + 2].reshape(2 * BLK, tv.shape[2])
        for n in range(nocc // 256):
            cols = slice(n * 256, (n + 1) * 256)
            r = jnp.dot(lhs, cv[:, cols], preferred_element_type=jnp.float32).astype(jnp.bfloat16)
            h[core, t, 0, :, cols] = r[:BLK]
            h[core, t, 1, :, cols] = r[BLK:]
        if t == 0:
            pl.semaphore_wait(barrier, 24 - 4 * (z // 8))
        for d in range(2):
            hop(d, t).start()
        for d in range(2):
            to_partner(t, d).start()

    def dot_nt(a, b):
        return lax.dot_general(a, b, NT, preferred_element_type=jnp.float32)

    for t in range(2):
        for d in range(2):
            to_partner(t, d).wait_recv()
    for who, put in ((core, blk0), (other, far0)):
        total = None
        for t in range(2):
            for d in range(2):
                v = dot_nt(h[who, t, d], h[core, t, d])
                total = v if total is None else total + v
        put[2] = total

    def pair(who, t, d, slot, rows_own):
        a, b = h[who, t, d], ring[d, slot]
        return dot_nt(a, b) if rows_own else dot_nt(b, a)

    def ring_step(s, t):
        slot = 2 * (s - 1) + t
        for d in range(2):
            hop(d, slot).wait_recv()
            if slot < 4:
                hop(d, slot + 2).start()
            elif slot == 5:
                hop(d, 6).start()
        for d in range(2):
            own = pair(core, t, d, slot, d == 0)
            away = pair(other, t, d, slot, d == 0)
            if t == 0:
                blk[s - 1][d] = own
                far[s - 1][d] = away
            else:
                blk[s - 1][d] += own
                far[s - 1][d] += away

    def antipode():
        for d in range(2):
            hop(d, 6).wait_recv()

        for side in range(2):
            @pl.when(high == side)
            def _():
                blk[3][0] = pair(core, side, 0, 6, side == 0) + pair(core, side, 1, 6, side == 0)
                far[3][0] = pair(other, side, 0, 6, side == 0) + pair(other, side, 1, 6, side == 0)

    def wait_bytes(ref, sem):
        pltpu.make_async_copy(ref, ref, sem).wait()

    def quarter(xx):
        return pl.ds(pl.multiple_of(xx * QUART, QUART), QUART)

    def when_owner(g, fn):
        if OWNERS[g] == Z:
            fn()
        else:
            pl.when(z < OWNERS[g])(fn)

    def when_mirrored(fn):
        pl.when(z < 8)(fn)

    def xrs_start(g):
        for d in range(X):
            q = quarter((x + d) % X)
            if d:
                remote(blk[g].at[:, q, :], xa[g].at[d - 1], xs_s.at[g], xs_r.at[g], x_peer(d, core)).start()
            remote(far[g].at[:, q, :], xb[g].at[d], xt_s.at[g], xt_r.at[g], x_peer(d, other)).start()

    def tile(ref, g, zz, first=0):
        sign, k, row = tile_of(g, zz)
        return ref.at[k, sign, pl.ds(pl.multiple_of(first + row, TILE[g]), TILE[g]), :]

    def zrs_start(g):
        wait_bytes(xa[g], xs_r.at[g])
        wait_bytes(xb[g], xt_r.at[g])
        xs[g][core] = (blk[g][:, quarter(x), :] + xa[g][0]) + (xa[g][1] + xa[g][2])
        xs[g][other] = (xb[g][0] + xb[g][1]) + (xb[g][2] + xb[g][3])

        @pl.loop(1, Z)
        def _(d):
            zz = (z + d) % Z

            def send():
                remote(tile(xs[g], g, zz), zr[g].at[d - 1], zs_s.at[g], zs_r.at[g], z_peer(d)).start()

            if OWNERS[g] == Z:
                send()
            else:
                pl.when(zz < OWNERS[g])(send)

    def exchange(g):
        return remote(zt[g], ze[g], e_s.at[g], e_r.at[g], mirror(g))

    def ex_start(g):
        def collect():
            wait_bytes(zr[g], zs_r.at[g])
            total = tile(xs[g], g, z)[...]
            for d in range(Z - 1):
                total = total + zr[g][d]
            zt[g][...] = total

        when_owner(g, collect)
        when_mirrored(lambda: exchange(g).start())

    def zag_start(g):
        @pl.when(z < 8)
        def _():
            exchange(g).wait_recv()
            tile(full[g], g, z, x * QUART)[...] = zt[g][...] + ze[g][...]

        if g == 0:
            @pl.when(z >= 8)
            def _():
                tile(full[g], g, z, x * QUART)[...] = zt[g][...]

        def spread_out():
            @pl.loop(1, Z)
            def _(d):
                mine = tile(full[g], g, z, x * QUART)
                remote(mine, mine, zg_s.at[g], zg_r.at[g], z_peer(d)).start()

        when_owner(g, spread_out)

    def x_slab(g):
        return full[g].at[:, :, quarter(x), :]

    def three_quarters(g):
        return full[g].at[:, :, pl.ds(0, 3 * QUART), :]

    def xag_start(g):
        if OWNERS[g] == Z:
            wait_bytes(zr[g], zg_r.at[g])
        else:
            @pl.when(z < OWNERS[g])
            def _():
                wait_bytes(zr[g].at[pl.ds(0, OWNERS[g] - 1)], zg_r.at[g])

            @pl.when(z >= OWNERS[g])
            def _():
                wait_bytes(zr[g].at[pl.ds(0, OWNERS[g])], zg_r.at[g])
        if g == 3:
            for d in range(1, X):
                remote(x_slab(g), x_slab(g), xg_s.at[g], xg_r.at[g, 0], x_peer(d, core)).start()
        else:
            for side in range(2):
                x_first(g, side).start()

    def x_first(g, side):
        return remote(x_slab(g), x_slab(g), xg_s.at[g], xg_r.at[g, side], x_peer(X - 1 if side else 1, core))

    def x_second(g, side):
        start = ((x + (1 if side else X - 1)) % X) * QUART + side * (QUART // 2)
        part = full[g].at[:, :, pl.ds(pl.multiple_of(start, QUART // 2), QUART // 2), :]
        return remote(part, part, xh_s.at[g], xg_r.at[g, 2 + side], x_peer(X - 1 if side else 1, core))

    def xag_forward(g):
        for side in range(2):
            x_first(g, side).wait_recv()
            x_second(g, side).start()

    def put(d, k, value):
        out_ref[:, pl.ds(pl.multiple_of((2 * d + k) * BLK, BLK), BLK)] = value

    def finish(g):
        if g == 3:
            wait_bytes(three_quarters(g), xg_r.at[g, 0])
        else:
            for side in range(2):
                x_second(g, side).wait_recv()
        s = g + 1
        if g < 3:
            for k in range(2):
                put((y + s) % Y, k, full[g][k, 0])
                put((y + Y - s) % Y, k, full[g][k, 1].T)
                if g == 0:
                    put(y, k, full[g][k, 2])
        else:
            for side in range(2):
                @pl.when(high == side)
                def _():
                    for k in range(2):
                        v = full[g][k, 0]
                        put((y + 4) % Y, k, v if side == 0 else v.T)

    ring_step(1, 0)
    ring_step(1, 1)
    xrs_start(0)
    ring_step(2, 0)
    zrs_start(0)
    ring_step(2, 1)
    xrs_start(1)
    ring_step(3, 0)
    ex_start(0)
    zrs_start(1)
    ring_step(3, 1)
    xrs_start(2)
    zag_start(0)
    antipode()
    xrs_start(3)
    ex_start(1)
    xag_start(0)
    zrs_start(2)
    zag_start(1)
    zrs_start(3)
    xag_forward(0)
    ex_start(2)
    xag_start(1)
    ex_start(3)
    finish(0)
    zag_start(2)
    xag_forward(1)
    zag_start(3)
    xag_start(2)
    finish(1)
    xag_start(3)
    xag_forward(2)
    finish(2)
    finish(3)

    for t in range(2):
        for d in range(2):
            to_partner(t, d).wait_send()
    for d in range(2):
        for slot in range(7):
            hop(d, slot).wait_send()
    for g in range(GROUPS):
        wait_bytes(xa[g], xs_s.at[g])
        wait_bytes(xb[g], xt_s.at[g])
        if OWNERS[g] == Z:
            wait_bytes(zr[g], zs_s.at[g])
            wait_bytes(zr[g], zg_s.at[g])
        else:
            @pl.when(z < OWNERS[g])
            def _():
                wait_bytes(zr[g].at[pl.ds(0, OWNERS[g] - 1)], zs_s.at[g])
                wait_bytes(zr[g], zg_s.at[g])

            @pl.when(z >= OWNERS[g])
            def _():
                wait_bytes(zr[g].at[pl.ds(0, OWNERS[g])], zs_s.at[g])
        when_mirrored(lambda: exchange(g).wait_send())
        if g == 3:
            wait_bytes(three_quarters(g), xg_s.at[g])
        else:
            wait_bytes(full[g].at[:, :, pl.ds(0, 2 * QUART), :], xg_s.at[g])
            wait_bytes(full[g].at[:, :, pl.ds(0, QUART), :], xh_s.at[g])


def on_device(three_centre, screening, coefficients, occ_pattern):
    nocc = coefficients.shape[1]
    norb = coefficients.shape[0]
    bf, f32 = jnp.bfloat16, jnp.float32
    dma = pltpu.SemaphoreType.DMA
    vmem = pltpu.VMEM
    return pl.pallas_call(
        kernel,
        out_shape=jax.ShapeDtypeStruct((BLK, norb), f32),
        in_specs=[pl.BlockSpec(memory_space=pl.ANY)] * 4,
        out_specs=pl.BlockSpec(memory_space=vmem),
        scratch_shapes=[
            vmem((4, BLK, norb), bf),
            vmem((norb, nocc), bf),
            vmem(screening.shape, jnp.int32),
            vmem(occ_pattern.shape, jnp.int32),
            vmem((2, 2, 2, BLK, nocc), bf),
            vmem((2, 7, BLK, nocc), bf),
            *[vmem((n, BLK, BLK), f32) for n in SIGNS],
            *[vmem((n, BLK, BLK), f32) for n in SIGNS],
            *[vmem((X - 1, n, QUART, BLK), f32) for n in SIGNS],
            *[vmem((X, n, QUART, BLK), f32) for n in SIGNS],
            *[vmem((2, n, QUART, BLK), f32) for n in SIGNS],
            *[vmem((Z - 1, r, BLK), f32) for r in TILE],
            *[vmem((r, BLK), f32) for r in TILE],
            *[vmem((r, BLK), f32) for r in TILE],
            *[vmem((2, n, BLK, BLK), f32) for n in SIGNS],
            dma((10,)),
            dma((2, 2)), dma((2, 2)),
            dma((2, 7)), dma((2, 7)),
            *[dma((GROUPS,))] * 12,
            dma((GROUPS, 4)),
        ],
        compiler_params=pltpu.CompilerParams(
            collective_id=0, has_side_effects=True, vmem_limit_bytes=60 * 2**20),
        cost_estimate=pl.CostEstimate(flops=3 * 10**9, bytes_accessed=6 * 10**6, transcendentals=0),
    )(three_centre, screening, coefficients, occ_pattern)


def solution(mesh):
    return jax.shard_map(
        on_device,
        mesh=mesh,
        in_specs=(P("aux", "orb", None), P("aux", "orb", None), P(), P()),
        out_specs=P("orb", None),
        check_vma=False,
    )
```

```python
import jax
import jax.numpy as jnp
from jax import lax
from jax.experimental import pallas as pl
from jax.experimental.pallas import tpu as pltpu
from jax.sharding import PartitionSpec as P

MESH = pl.DeviceIdType.MESH
X, Y, Z = 4, 8, 12
BLK = 128
NT = (((1,), (1,)), ((), ()))


SIGNS = (3, 2, 2, 1)
TILE = (16, 16, 16, 8)
OWNERS = (12, 8, 8, 8)
GROUPS = len(SIGNS)
QUART = BLK // X


def kernel(t_hbm, c_hbm, switch_ref, out_ref,
           tv, cv, h, ring,
           blk0, blk1, blk2, blk3,
           xa0, xa1, xa2, xa3, xb0, xb1, xb2, xb3, xs0, xs1, xs2, xs3,
           zr0, zr1, zr2, zr3, zt0, zt1, zt2, zt3, ze0, ze1, ze2, ze3,
           full0, full1, full2, full3,
           load_sem, part_s, part_r, ring_s, ring_r,
           xs_s, xs_r, xt_s, xt_r, zs_s, zs_r, e_s, e_r, zg_s, zg_r, xg_s, xg_r):
    blk = (blk0, blk1, blk2, blk3)
    xa, xb, xs = (xa0, xa1, xa2, xa3), (xb0, xb1, xb2, xb3), (xs0, xs1, xs2, xs3)
    zr, zt, ze = (zr0, zr1, zr2, zr3), (zt0, zt1, zt2, zt3), (ze0, ze1, ze2, ze3)
    full = (full0, full1, full2, full3)
    aux = lax.axis_index("aux")
    orb = lax.axis_index("orb")
    x, z = aux // Z, aux % Z
    y, core = orb // 2, orb % 2
    other = 1 - core
    high = y // 4
    nocc = cv.shape[1]

    def dev(xx, zz, yy, cc):
        return (xx * Z + zz, yy * 2 + cc)

    def remote(src, dst, s_sem, r_sem, where):
        return pltpu.make_async_remote_copy(
            src_ref=src, dst_ref=dst, send_sem=s_sem, recv_sem=r_sem,
            device_id=where, device_id_type=MESH)

    partner = dev(x, z, y, other)
    nexts = (dev(x, z, (y + Y - 1) % Y, core), dev(x, z, (y + 1) % Y, core))

    def tile_of(g, zz):
        if g == 3:
            return 0, (zz // 4 + core) % 2, (zz % 4) * TILE[g]
        a, b, part = zz // 4, (zz // 2) % 2, zz % 2
        flip = (a + (y // 2 if g == 1 else y)) % 2
        sign = (1 - a // 2) * flip + (a // 2) * 2 if g == 0 else flip
        return sign, (b + core) % 2, part * TILE[g]

    def mirror(g):
        sign, k, _ = tile_of(g, z)
        dy = 4 if g == 3 else (1 - sign) * (g + 1) + sign * (Y - g - 1)
        return dev(x, z, (y + dy) % Y, k)

    def x_peer(d, cc):
        return dev((x + d) % X, z, y, cc)

    def z_peer(d):
        return dev(x, (z + d) % Z, y, core)

    def load_t(p):
        return pltpu.make_async_copy(t_hbm.at[p], tv.at[p], load_sem.at[p])

    crows = cv.shape[0] // 4

    def load_c(q):
        rows = pl.ds(q * crows, crows)
        return pltpu.make_async_copy(c_hbm.at[rows], cv.at[rows], load_sem.at[4 + q])

    for q in range(4):
        load_c(q).start()
    for p in range(4):
        load_t(p).start()

    barrier = pltpu.get_barrier_semaphore()

    def signal(where):
        pl.semaphore_signal(barrier, inc=1, device_id=where, device_id_type=MESH)

    signal(partner)
    signal(nexts[0])
    signal(nexts[1])
    for d in range(X):
        if d:
            signal(x_peer(d, core))
            signal(x_peer(d, other))

    @pl.loop(1, Z)
    def _(d):
        signal(z_peer(d))

    @pl.when(z < 8)
    def _():
        for g in range(GROUPS):
            signal(mirror(g))

    switches = switch_ref[...]
    occ = switches[:16].astype(jnp.float32).astype(jnp.bfloat16)
    nslices = occ.shape[1]
    spread = (lax.broadcasted_iota(jnp.int32, (nslices, nocc), 1) // (nocc // nslices)
              == lax.broadcasted_iota(jnp.int32, (nslices, nocc), 0)).astype(jnp.float32).astype(jnp.bfloat16)
    occ_mask = jnp.dot(occ, spread, preferred_element_type=jnp.float32).astype(jnp.bfloat16)
    screen = switches[16:20, :16].astype(jnp.float32).astype(jnp.bfloat16)
    widen = (lax.broadcasted_iota(jnp.int32, (16, 2048), 1) // BLK
             == lax.broadcasted_iota(jnp.int32, (16, 2048), 0)).astype(jnp.float32).astype(jnp.bfloat16)
    scr_mask = jnp.dot(screen, widen, preferred_element_type=jnp.float32).astype(jnp.bfloat16)

    for q in range(4):
        load_c(q).wait()
        for nb in range(4 * q, 4 * q + 4):
            rows = slice(nb * BLK, (nb + 1) * BLK)
            cv[rows, :] = cv[rows, :] * occ_mask[nb:nb + 1, :]

    def hop(d, slot):
        if slot < 2:
            src = h.at[core, slot, d]
        elif slot < 6:
            src = ring.at[d, slot - 2]
        else:
            target = (y + Y - 1) % Y if d == 0 else (y + 1) % Y
            src = ring.at[d, 4 + target // 4]
        return remote(src, ring.at[d, slot], ring_s.at[d, slot], ring_r.at[d, slot], nexts[d])

    def to_partner(t, d):
        return remote(h.at[core, t, d], h.at[core, t, d], part_s.at[t, d], part_r.at[t, d], partner)

    for t in range(2):
        for p in (2 * t, 2 * t + 1):
            load_t(p).wait()
            tv[p] = tv[p] * scr_mask[p:p + 1, :]
        lhs = tv[2 * t:2 * t + 2].reshape(2 * BLK, tv.shape[2])
        for n in range(nocc // 256):
            cols = slice(n * 256, (n + 1) * 256)
            r = jnp.dot(lhs, cv[:, cols], preferred_element_type=jnp.float32).astype(jnp.bfloat16)
            h[core, t, 0, :, cols] = r[:BLK]
            h[core, t, 1, :, cols] = r[BLK:]
        if t == 0:
            pl.semaphore_wait(barrier, 24 - 4 * (z // 8))
        for d in range(2):
            hop(d, t).start()
        for d in range(2):
            to_partner(t, d).start()

    def dot_nt(a, b):
        return lax.dot_general(a, b, NT, preferred_element_type=jnp.float32)

    for t in range(2):
        for d in range(2):
            to_partner(t, d).wait_recv()
    def chip_rows(t, d):
        return h[:, t, d].reshape(2 * BLK, nocc)

    total = None
    for t in range(2):
        for d in range(2):
            v = dot_nt(chip_rows(t, d), h[core, t, d])
            total = v if total is None else total + v
    blk[0][0, 2] = total[:BLK]
    blk[0][1, 2] = total[BLK:]

    def pair(t, d, slot, rows_own):
        a, b = chip_rows(t, d), ring[d, slot]
        if rows_own:
            r = dot_nt(a, b)
            return r[:BLK], r[BLK:]
        r = dot_nt(b, a)
        return r[:, :BLK], r[:, BLK:]

    def ring_step(s, t):
        slot = 2 * (s - 1) + t
        for d in range(2):
            hop(d, slot).wait_recv()
            if slot < 4:
                hop(d, slot + 2).start()
            elif slot == 5:
                hop(d, 6).start()
        for d in range(2):
            parts = pair(t, d, slot, d == 0)
            for who in range(2):
                if t == 0:
                    blk[s - 1][who, d] = parts[who]
                else:
                    blk[s - 1][who, d] += parts[who]

    def antipode():
        for d in range(2):
            hop(d, 6).wait_recv()

        for side in range(2):
            @pl.when(high == side)
            def _():
                left = pair(side, 0, 6, side == 0)
                right = pair(side, 1, 6, side == 0)
                for who in range(2):
                    blk[3][who, 0] = left[who] + right[who]

    def wait_bytes(ref, sem):
        pltpu.make_async_copy(ref, ref, sem).wait()

    def quarter(xx):
        return pl.ds(pl.multiple_of(xx * QUART, QUART), QUART)

    def when_owner(g, fn):
        if OWNERS[g] == Z:
            fn()
        else:
            pl.when(z < OWNERS[g])(fn)

    def when_mirrored(fn):
        pl.when(z < 8)(fn)

    def xrs_start(g):
        for d in range(X):
            q = quarter((x + d) % X)
            if d:
                remote(blk[g].at[core, :, q, :], xa[g].at[d - 1], xs_s.at[g], xs_r.at[g], x_peer(d, core)).start()
            remote(blk[g].at[other, :, q, :], xb[g].at[d], xt_s.at[g], xt_r.at[g], x_peer(d, other)).start()

    def tile(ref, g, zz, first=0):
        sign, k, row = tile_of(g, zz)
        return ref.at[k, sign, pl.ds(pl.multiple_of(first + row, TILE[g]), TILE[g]), :]

    def zrs_start(g):
        wait_bytes(xa[g], xs_r.at[g])
        wait_bytes(xb[g], xt_r.at[g])
        xs[g][core] = (blk[g][core, :, quarter(x), :] + xa[g][0]) + (xa[g][1] + xa[g][2])
        xs[g][other] = (xb[g][0] + xb[g][1]) + (xb[g][2] + xb[g][3])

        @pl.loop(1, Z)
        def _(d):
            zz = (z + d) % Z

            def send():
                remote(tile(xs[g], g, zz), zr[g].at[d - 1], zs_s.at[g], zs_r.at[g], z_peer(d)).start()

            if OWNERS[g] == Z:
                send()
            else:
                pl.when(zz < OWNERS[g])(send)

    def exchange(g):
        return remote(zt[g], ze[g], e_s.at[g], e_r.at[g], mirror(g))

    def ex_start(g):
        def collect():
            wait_bytes(zr[g], zs_r.at[g])
            total = tile(xs[g], g, z)[...]
            for d in range(Z - 1):
                total = total + zr[g][d]
            zt[g][...] = total

        when_owner(g, collect)
        when_mirrored(lambda: exchange(g).start())

    def zag_start(g):
        @pl.when(z < 8)
        def _():
            exchange(g).wait_recv()
            tile(full[g], g, z, x * QUART)[...] = zt[g][...] + ze[g][...]

        if g == 0:
            @pl.when(z >= 8)
            def _():
                tile(full[g], g, z, x * QUART)[...] = zt[g][...]

        def spread_out():
            @pl.loop(1, Z)
            def _(d):
                mine = tile(full[g], g, z, x * QUART)
                remote(mine, mine, zg_s.at[g], zg_r.at[g], z_peer(d)).start()

        when_owner(g, spread_out)

    def x_slab(g):
        return full[g].at[:, :, quarter(x), :]

    def three_quarters(g):
        return full[g].at[:, :, pl.ds(0, 3 * QUART), :]

    def xag_start(g):
        if OWNERS[g] == Z:
            wait_bytes(zr[g], zg_r.at[g])
        else:
            @pl.when(z < OWNERS[g])
            def _():
                wait_bytes(zr[g].at[pl.ds(0, OWNERS[g] - 1)], zg_r.at[g])

            @pl.when(z >= OWNERS[g])
            def _():
                wait_bytes(zr[g].at[pl.ds(0, OWNERS[g])], zg_r.at[g])
        for d in range(1, X):
            remote(x_slab(g), x_slab(g), xg_s.at[g], xg_r.at[g], x_peer(d, core)).start()

    def put(d, k, value):
        out_ref[:, pl.ds(pl.multiple_of((2 * d + k) * BLK, BLK), BLK)] = value

    def finish(g):
        wait_bytes(three_quarters(g), xg_r.at[g])
        s = g + 1
        if g < 3:
            for k in range(2):
                put((y + s) % Y, k, full[g][k, 0])
                put((y + Y - s) % Y, k, full[g][k, 1].T)
                if g == 0:
                    put(y, k, full[g][k, 2])
        else:
            for side in range(2):
                @pl.when(high == side)
                def _():
                    for k in range(2):
                        v = full[g][k, 0]
                        put((y + 4) % Y, k, v if side == 0 else v.T)

    ring_step(1, 0)
    ring_step(1, 1)
    xrs_start(0)
    ring_step(2, 0)
    zrs_start(0)
    ring_step(2, 1)
    xrs_start(1)
    ring_step(3, 0)
    ex_start(0)
    zrs_start(1)
    ring_step(3, 1)
    xrs_start(2)
    zag_start(0)
    antipode()
    xrs_start(3)
    ex_start(1)
    zrs_start(2)
    xag_start(0)
    zag_start(1)
    zrs_start(3)
    ex_start(2)
    xag_start(1)
    zag_start(2)
    ex_start(3)
    finish(0)
    zag_start(3)
    finish(1)
    xag_start(2)
    xag_start(3)
    finish(2)
    finish(3)

    for t in range(2):
        for d in range(2):
            to_partner(t, d).wait_send()
    for d in range(2):
        for slot in range(7):
            hop(d, slot).wait_send()
    for g in range(GROUPS):
        wait_bytes(xa[g], xs_s.at[g])
        wait_bytes(xb[g], xt_s.at[g])
        if OWNERS[g] == Z:
            wait_bytes(zr[g], zs_s.at[g])
            wait_bytes(zr[g], zg_s.at[g])
        else:
            @pl.when(z < OWNERS[g])
            def _():
                wait_bytes(zr[g].at[pl.ds(0, OWNERS[g] - 1)], zs_s.at[g])
                wait_bytes(zr[g], zg_s.at[g])

            @pl.when(z >= OWNERS[g])
            def _():
                wait_bytes(zr[g].at[pl.ds(0, OWNERS[g])], zs_s.at[g])
        when_mirrored(lambda: exchange(g).wait_send())
        wait_bytes(three_quarters(g), xg_s.at[g])


def on_device(three_centre, screening, coefficients, occ_pattern):
    nocc = coefficients.shape[1]
    norb = coefficients.shape[0]
    bf, f32 = jnp.bfloat16, jnp.float32
    dma = pltpu.SemaphoreType.DMA
    vmem = pltpu.VMEM
    nslices = occ_pattern.shape[1]
    switches = jnp.concatenate(
        [occ_pattern, jnp.pad(screening[:, 0, :], ((0, 4), (0, nslices - screening.shape[2])))], axis=0)
    return pl.pallas_call(
        kernel,
        out_shape=jax.ShapeDtypeStruct((BLK, norb), f32),
        in_specs=[pl.BlockSpec(memory_space=pl.ANY)] * 2 + [pl.BlockSpec(memory_space=vmem)],
        out_specs=pl.BlockSpec(memory_space=vmem),
        scratch_shapes=[
            vmem((4, BLK, norb), bf),
            vmem((norb, nocc), bf),
            vmem((2, 2, 2, BLK, nocc), bf),
            vmem((2, 7, BLK, nocc), bf),
            *[vmem((2, n, BLK, BLK), f32) for n in SIGNS],
            *[vmem((X - 1, n, QUART, BLK), f32) for n in SIGNS],
            *[vmem((X, n, QUART, BLK), f32) for n in SIGNS],
            *[vmem((2, n, QUART, BLK), f32) for n in SIGNS],
            *[vmem((Z - 1, r, BLK), f32) for r in TILE],
            *[vmem((r, BLK), f32) for r in TILE],
            *[vmem((r, BLK), f32) for r in TILE],
            *[vmem((2, n, BLK, BLK), f32) for n in SIGNS],
            dma((8,)),
            dma((2, 2)), dma((2, 2)),
            dma((2, 7)), dma((2, 7)),
            *[dma((GROUPS,))] * 12,
        ],
        compiler_params=pltpu.CompilerParams(
            collective_id=0, has_side_effects=True, vmem_limit_bytes=52 * 2**20),
        cost_estimate=pl.CostEstimate(flops=3 * 10**9, bytes_accessed=6 * 10**6, transcendentals=0),
    )(three_centre, coefficients, switches)


def solution(mesh):
    return jax.shard_map(
        on_device,
        mesh=mesh,
        in_specs=(P("aux", "orb", None), P("aux", "orb", None), P(), P()),
        out_specs=P("orb", None),
        check_vma=False,
    )
```

```python
import jax
import jax.numpy as jnp
from jax import lax
from jax.experimental import pallas as pl
from jax.experimental.pallas import tpu as pltpu
from jax.sharding import PartitionSpec as P

MESH = pl.DeviceIdType.MESH
X, Y, Z = 4, 8, 12
BLK = 128
NT = (((1,), (1,)), ((), ()))


SIGNS = (3, 2, 2, 1)
TILE = (16, 16, 16, 8)
OWNERS = (12, 8, 8, 8)
GROUPS = len(SIGNS)
QUART = BLK // X


def kernel(t_hbm, c_hbm, switch_ref, out_ref,
           tv, cv, h, ring,
           blk0, blk1, blk2, blk3,
           xa0, xa1, xa2, xa3, xb0, xb1, xb2, xb3, xs0, xs1, xs2, xs3,
           zr0, zr1, zr2, zr3, zt0, zt1, zt2, zt3, ze0, ze1, ze2, ze3,
           full0, full1, full2, full3,
           load_sem, part_s, part_r, ring_s, ring_r,
           xs_s, xs_r, xt_s, xt_r, zs_s, zs_r, e_s, e_r, zg_s, zg_r, xg_s, xg_r):
    blk = (blk0, blk1, blk2, blk3)
    xa, xb, xs = (xa0, xa1, xa2, xa3), (xb0, xb1, xb2, xb3), (xs0, xs1, xs2, xs3)
    zr, zt, ze = (zr0, zr1, zr2, zr3), (zt0, zt1, zt2, zt3), (ze0, ze1, ze2, ze3)
    full = (full0, full1, full2, full3)
    aux = lax.axis_index("aux")
    orb = lax.axis_index("orb")
    x, z = aux // Z, aux % Z
    y, core = orb // 2, orb % 2
    other = 1 - core
    high = y // 4
    nocc = cv.shape[1]

    def dev(xx, zz, yy, cc):
        return (xx * Z + zz, yy * 2 + cc)

    def remote(src, dst, s_sem, r_sem, where):
        return pltpu.make_async_remote_copy(
            src_ref=src, dst_ref=dst, send_sem=s_sem, recv_sem=r_sem,
            device_id=where, device_id_type=MESH)

    partner = dev(x, z, y, other)
    nexts = (dev(x, z, (y + Y - 1) % Y, core), dev(x, z, (y + 1) % Y, core))

    def tile_of(g, zz):
        if g == 3:
            return 0, (zz // 4 + core) % 2, (zz % 4) * TILE[g]
        a, b, part = zz // 4, (zz // 2) % 2, zz % 2
        flip = (a + (y // 2 if g == 1 else y)) % 2
        sign = (1 - a // 2) * flip + (a // 2) * 2 if g == 0 else flip
        return sign, (b + core) % 2, part * TILE[g]

    def mirror(g):
        sign, k, _ = tile_of(g, z)
        dy = 4 if g == 3 else (1 - sign) * (g + 1) + sign * (Y - g - 1)
        return dev(x, z, (y + dy) % Y, k)

    def x_peer(d, cc):
        return dev((x + d) % X, z, y, cc)

    def z_peer(d):
        return dev(x, (z + d) % Z, y, core)

    def far_first(i):
        return Z // 2 + (2 * (i % 2) - 1) * ((i + 1) // 2)

    def load_t(p):
        return pltpu.make_async_copy(t_hbm.at[p], tv.at[p], load_sem.at[p])

    crows = cv.shape[0] // 4

    def load_c(q):
        rows = pl.ds(q * crows, crows)
        return pltpu.make_async_copy(c_hbm.at[rows], cv.at[rows], load_sem.at[4 + q])

    for q in range(4):
        load_c(q).start()
    for p in range(4):
        load_t(p).start()

    barrier = pltpu.get_barrier_semaphore()

    def signal(where):
        pl.semaphore_signal(barrier, inc=1, device_id=where, device_id_type=MESH)

    signal(partner)
    signal(nexts[0])
    signal(nexts[1])
    for d in range(X):
        if d:
            signal(x_peer(d, core))
            signal(x_peer(d, other))

    @pl.loop(1, Z)
    def _(d):
        signal(z_peer(d))

    @pl.when(z < 8)
    def _():
        for g in range(GROUPS):
            signal(mirror(g))

    switches = switch_ref[...]
    occ = switches[:16].astype(jnp.float32).astype(jnp.bfloat16)
    nslices = occ.shape[1]
    spread = (lax.broadcasted_iota(jnp.int32, (nslices, nocc), 1) // (nocc // nslices)
              == lax.broadcasted_iota(jnp.int32, (nslices, nocc), 0)).astype(jnp.float32).astype(jnp.bfloat16)
    occ_mask = jnp.dot(occ, spread, preferred_element_type=jnp.float32).astype(jnp.bfloat16)
    screen = switches[16:20, :16].astype(jnp.float32).astype(jnp.bfloat16)
    widen = (lax.broadcasted_iota(jnp.int32, (16, 2048), 1) // BLK
             == lax.broadcasted_iota(jnp.int32, (16, 2048), 0)).astype(jnp.float32).astype(jnp.bfloat16)
    scr_mask = jnp.dot(screen, widen, preferred_element_type=jnp.float32).astype(jnp.bfloat16)

    for q in range(4):
        load_c(q).wait()
        for nb in range(4 * q, 4 * q + 4):
            rows = slice(nb * BLK, (nb + 1) * BLK)
            cv[rows, :] = cv[rows, :] * occ_mask[nb:nb + 1, :]

    def hop(d, slot):
        if slot < 2:
            src = h.at[core, slot, d]
        elif slot < 6:
            src = ring.at[d, slot - 2]
        else:
            target = (y + Y - 1) % Y if d == 0 else (y + 1) % Y
            src = ring.at[d, 4 + target // 4]
        return remote(src, ring.at[d, slot], ring_s.at[d, slot], ring_r.at[d, slot], nexts[d])

    def to_partner(t, d):
        return remote(h.at[core, t, d], h.at[core, t, d], part_s.at[t, d], part_r.at[t, d], partner)

    for t in range(2):
        for p in (2 * t, 2 * t + 1):
            load_t(p).wait()
            tv[p] = tv[p] * scr_mask[p:p + 1, :]
        lhs = tv[2 * t:2 * t + 2].reshape(2 * BLK, tv.shape[2])
        for n in range(nocc // 256):
            cols = slice(n * 256, (n + 1) * 256)
            r = jnp.dot(lhs, cv[:, cols], preferred_element_type=jnp.float32).astype(jnp.bfloat16)
            h[core, t, 0, :, cols] = r[:BLK]
            h[core, t, 1, :, cols] = r[BLK:]
        if t == 0:
            pl.semaphore_wait(barrier, 24 - 4 * (z // 8))
        for d in range(2):
            hop(d, t).start()
        for d in range(2):
            to_partner(t, d).start()

    def dot_nt(a, b):
        return lax.dot_general(a, b, NT, preferred_element_type=jnp.float32)

    for t in range(2):
        for d in range(2):
            to_partner(t, d).wait_recv()
    def chip_rows(t, d):
        return h[:, t, d].reshape(2 * BLK, nocc)

    total = None
    for t in range(2):
        for d in range(2):
            v = dot_nt(chip_rows(t, d), h[core, t, d])
            total = v if total is None else total + v
    blk[0][0, 2] = total[:BLK]
    blk[0][1, 2] = total[BLK:]

    def pair(t, d, slot, rows_own):
        a, b = chip_rows(t, d), ring[d, slot]
        if rows_own:
            r = dot_nt(a, b)
            return r[:BLK], r[BLK:]
        r = dot_nt(b, a)
        return r[:, :BLK], r[:, BLK:]

    def ring_step(s, t):
        slot = 2 * (s - 1) + t
        for d in range(2):
            hop(d, slot).wait_recv()
            if slot < 4:
                hop(d, slot + 2).start()
            elif slot == 5:
                hop(d, 6).start()
        for d in range(2):
            parts = pair(t, d, slot, d == 0)
            for who in range(2):
                if t == 0:
                    blk[s - 1][who, d] = parts[who]
                else:
                    blk[s - 1][who, d] += parts[who]

    def antipode():
        for d in range(2):
            hop(d, 6).wait_recv()

        for side in range(2):
            @pl.when(high == side)
            def _():
                left = pair(side, 0, 6, side == 0)
                right = pair(side, 1, 6, side == 0)
                for who in range(2):
                    blk[3][who, 0] = left[who] + right[who]

    def wait_bytes(ref, sem):
        pltpu.make_async_copy(ref, ref, sem).wait()

    def quarter(xx):
        return pl.ds(pl.multiple_of(xx * QUART, QUART), QUART)

    def when_owner(g, fn):
        if OWNERS[g] == Z:
            fn()
        else:
            pl.when(z < OWNERS[g])(fn)

    def when_mirrored(fn):
        pl.when(z < 8)(fn)

    def xrs_start(g):
        for d in (2, 1, 3, 0):
            q = quarter((x + d) % X)
            if d:
                remote(blk[g].at[core, :, q, :], xa[g].at[d - 1], xs_s.at[g], xs_r.at[g], x_peer(d, core)).start()
            remote(blk[g].at[other, :, q, :], xb[g].at[d], xt_s.at[g], xt_r.at[g], x_peer(d, other)).start()

    def tile(ref, g, zz, first=0):
        sign, k, row = tile_of(g, zz)
        return ref.at[k, sign, pl.ds(pl.multiple_of(first + row, TILE[g]), TILE[g]), :]

    def zrs_start(g):
        wait_bytes(xa[g], xs_r.at[g])
        wait_bytes(xb[g], xt_r.at[g])
        xs[g][core] = (blk[g][core, :, quarter(x), :] + xa[g][0]) + (xa[g][1] + xa[g][2])
        xs[g][other] = (xb[g][0] + xb[g][1]) + (xb[g][2] + xb[g][3])

        @pl.loop(0, Z - 1)
        def _(i):
            d = far_first(i)
            zz = (z + d) % Z

            def send():
                remote(tile(xs[g], g, zz), zr[g].at[d - 1], zs_s.at[g], zs_r.at[g], z_peer(d)).start()

            if OWNERS[g] == Z:
                send()
            else:
                pl.when(zz < OWNERS[g])(send)

    def exchange(g):
        return remote(zt[g], ze[g], e_s.at[g], e_r.at[g], mirror(g))

    def ex_start(g):
        def collect():
            wait_bytes(zr[g], zs_r.at[g])
            total = tile(xs[g], g, z)[...]
            for d in range(Z - 1):
                total = total + zr[g][d]
            zt[g][...] = total

        when_owner(g, collect)
        when_mirrored(lambda: exchange(g).start())

    def zag_start(g):
        @pl.when(z < 8)
        def _():
            exchange(g).wait_recv()
            tile(full[g], g, z, x * QUART)[...] = zt[g][...] + ze[g][...]

        if g == 0:
            @pl.when(z >= 8)
            def _():
                tile(full[g], g, z, x * QUART)[...] = zt[g][...]

        def spread_out():
            @pl.loop(0, Z - 1)
            def _(i):
                mine = tile(full[g], g, z, x * QUART)
                remote(mine, mine, zg_s.at[g], zg_r.at[g], z_peer(far_first(i))).start()

        when_owner(g, spread_out)

    def x_slab(g):
        return full[g].at[:, :, quarter(x), :]

    def three_quarters(g):
        return full[g].at[:, :, pl.ds(0, 3 * QUART), :]

    def xag_start(g):
        if OWNERS[g] == Z:
            wait_bytes(zr[g], zg_r.at[g])
        else:
            @pl.when(z < OWNERS[g])
            def _():
                wait_bytes(zr[g].at[pl.ds(0, OWNERS[g] - 1)], zg_r.at[g])

            @pl.when(z >= OWNERS[g])
            def _():
                wait_bytes(zr[g].at[pl.ds(0, OWNERS[g])], zg_r.at[g])
        for d in (2, 1, 3):
            remote(x_slab(g), x_slab(g), xg_s.at[g], xg_r.at[g], x_peer(d, core)).start()

    def put(d, k, value):
        out_ref[:, pl.ds(pl.multiple_of((2 * d + k) * BLK, BLK), BLK)] = value

    def finish(g):
        wait_bytes(three_quarters(g), xg_r.at[g])
        s = g + 1
        if g < 3:
            for k in range(2):
                put((y + s) % Y, k, full[g][k, 0])
                put((y + Y - s) % Y, k, full[g][k, 1].T)
                if g == 0:
                    put(y, k, full[g][k, 2])
        else:
            for side in range(2):
                @pl.when(high == side)
                def _():
                    for k in range(2):
                        v = full[g][k, 0]
                        put((y + 4) % Y, k, v if side == 0 else v.T)

    ring_step(1, 0)
    ring_step(1, 1)
    xrs_start(0)
    ring_step(2, 0)
    zrs_start(0)
    ring_step(2, 1)
    xrs_start(1)
    ring_step(3, 0)
    ex_start(0)
    zrs_start(1)
    ring_step(3, 1)
    xrs_start(2)
    zag_start(0)
    antipode()
    xrs_start(3)
    ex_start(1)
    zrs_start(2)
    xag_start(0)
    zag_start(1)
    zrs_start(3)
    ex_start(2)
    xag_start(1)
    zag_start(2)
    ex_start(3)
    finish(0)
    zag_start(3)
    finish(1)
    xag_start(2)
    xag_start(3)
    finish(2)
    finish(3)

    for t in range(2):
        for d in range(2):
            to_partner(t, d).wait_send()
    for d in range(2):
        for slot in range(7):
            hop(d, slot).wait_send()
    for g in range(GROUPS):
        wait_bytes(xa[g], xs_s.at[g])
        wait_bytes(xb[g], xt_s.at[g])
        if OWNERS[g] == Z:
            wait_bytes(zr[g], zs_s.at[g])
            wait_bytes(zr[g], zg_s.at[g])
        else:
            @pl.when(z < OWNERS[g])
            def _():
                wait_bytes(zr[g].at[pl.ds(0, OWNERS[g] - 1)], zs_s.at[g])
                wait_bytes(zr[g], zg_s.at[g])

            @pl.when(z >= OWNERS[g])
            def _():
                wait_bytes(zr[g].at[pl.ds(0, OWNERS[g])], zs_s.at[g])
        when_mirrored(lambda: exchange(g).wait_send())
        wait_bytes(three_quarters(g), xg_s.at[g])


def on_device(three_centre, screening, coefficients, occ_pattern):
    nocc = coefficients.shape[1]
    norb = coefficients.shape[0]
    bf, f32 = jnp.bfloat16, jnp.float32
    dma = pltpu.SemaphoreType.DMA
    vmem = pltpu.VMEM
    nslices = occ_pattern.shape[1]
    switches = jnp.concatenate(
        [occ_pattern, jnp.pad(screening[:, 0, :], ((0, 4), (0, nslices - screening.shape[2])))], axis=0)
    return pl.pallas_call(
        kernel,
        out_shape=jax.ShapeDtypeStruct((BLK, norb), f32),
        in_specs=[pl.BlockSpec(memory_space=pl.ANY)] * 2 + [pl.BlockSpec(memory_space=vmem)],
        out_specs=pl.BlockSpec(memory_space=vmem),
        scratch_shapes=[
            vmem((4, BLK, norb), bf),
            vmem((norb, nocc), bf),
            vmem((2, 2, 2, BLK, nocc), bf),
            vmem((2, 7, BLK, nocc), bf),
            *[vmem((2, n, BLK, BLK), f32) for n in SIGNS],
            *[vmem((X - 1, n, QUART, BLK), f32) for n in SIGNS],
            *[vmem((X, n, QUART, BLK), f32) for n in SIGNS],
            *[vmem((2, n, QUART, BLK), f32) for n in SIGNS],
            *[vmem((Z - 1, r, BLK), f32) for r in TILE],
            *[vmem((r, BLK), f32) for r in TILE],
            *[vmem((r, BLK), f32) for r in TILE],
            *[vmem((2, n, BLK, BLK), f32) for n in SIGNS],
            dma((8,)),
            dma((2, 2)), dma((2, 2)),
            dma((2, 7)), dma((2, 7)),
            *[dma((GROUPS,))] * 12,
        ],
        compiler_params=pltpu.CompilerParams(
            collective_id=0, has_side_effects=True, vmem_limit_bytes=52 * 2**20),
        cost_estimate=pl.CostEstimate(flops=3 * 10**9, bytes_accessed=6 * 10**6, transcendentals=0),
    )(three_centre, coefficients, switches)


def solution(mesh):
    return jax.shard_map(
        on_device,
        mesh=mesh,
        in_specs=(P("aux", "orb", None), P("aux", "orb", None), P(), P()),
        out_specs=P("orb", None),
        check_vma=False,
    )
```

```python
import jax
import jax.numpy as jnp
from jax import lax
from jax.experimental import pallas as pl
from jax.experimental.pallas import tpu as pltpu
from jax.sharding import PartitionSpec as P

MESH = pl.DeviceIdType.MESH
X, Y, Z = 4, 8, 12
BLK = 128
NT = (((1,), (1,)), ((), ()))


SIGNS = (3, 2, 2, 1)
TILE = (16, 16, 16, 8)
OWNERS = (12, 8, 8, 8)
SOURCES = (Z - 1, Z - 1, Z - 1, 2 * Z - 1)
GROUPS = len(SIGNS)
QUART = BLK // X


def kernel(t_hbm, c_hbm, switch_ref, out_ref,
           tv, cv, h, ring,
           blk0, blk1, blk2, blk3,
           xa0, xa1, xa2, xa3, xb0, xb1, xb2, xb3, xs0, xs1, xs2, xs3,
           zr0, zr1, zr2, zr3, zt0, zt1, zt2, zt3, ze0, ze1, ze2,
           full0, full1, full2, full3,
           load_sem, part_s, part_r, ring_s, ring_r,
           xs_s, xs_r, xt_s, xt_r, zs_s, zs_r, e_s, e_r, zg_s, zg_r, xg_s, xg_r):
    blk = (blk0, blk1, blk2, blk3)
    xa, xb, xs = (xa0, xa1, xa2, xa3), (xb0, xb1, xb2, xb3), (xs0, xs1, xs2, xs3)
    zr, zt, ze = (zr0, zr1, zr2, zr3), (zt0, zt1, zt2, zt3), (ze0, ze1, ze2)
    full = (full0, full1, full2, full3)
    aux = lax.axis_index("aux")
    orb = lax.axis_index("orb")
    x, z = aux // Z, aux % Z
    y, core = orb // 2, orb % 2
    other = 1 - core
    high = y // 4
    nocc = cv.shape[1]

    def dev(xx, zz, yy, cc):
        return (xx * Z + zz, yy * 2 + cc)

    def remote(src, dst, s_sem, r_sem, where):
        return pltpu.make_async_remote_copy(
            src_ref=src, dst_ref=dst, send_sem=s_sem, recv_sem=r_sem,
            device_id=where, device_id_type=MESH)

    partner = dev(x, z, y, other)
    nexts = (dev(x, z, (y + Y - 1) % Y, core), dev(x, z, (y + 1) % Y, core))

    def tile_of(g, zz):
        if g == 3:
            return 0, (zz // 4 + core) % 2, (zz % 4) * TILE[g]
        a, b, part = zz // 4, (zz // 2) % 2, zz % 2
        flip = (a + (y // 2 if g == 1 else y)) % 2
        sign = (1 - a // 2) * flip + (a // 2) * 2 if g == 0 else flip
        return sign, (b + core) % 2, part * TILE[g]

    def mirror(g):
        sign, k, _ = tile_of(g, z)
        dy = (1 - sign) * (g + 1) + sign * (Y - g - 1)
        return dev(x, z, (y + dy) % Y, k)

    def x_peer(d, cc):
        return dev((x + d) % X, z, y, cc)

    def z_peer(d):
        return dev(x, (z + d) % Z, y, core)

    def load_t(p):
        return pltpu.make_async_copy(t_hbm.at[p], tv.at[p], load_sem.at[p])

    crows = cv.shape[0] // 4

    def load_c(q):
        rows = pl.ds(q * crows, crows)
        return pltpu.make_async_copy(c_hbm.at[rows], cv.at[rows], load_sem.at[4 + q])

    for q in range(4):
        load_c(q).start()
    for p in range(4):
        load_t(p).start()

    barrier = pltpu.get_barrier_semaphore()

    def signal(where):
        pl.semaphore_signal(barrier, inc=1, device_id=where, device_id_type=MESH)

    signal(partner)
    signal(nexts[0])
    signal(nexts[1])
    for d in range(X):
        if d:
            signal(x_peer(d, core))
            signal(x_peer(d, other))

    @pl.loop(1, Z)
    def _(d):
        signal(z_peer(d))

    @pl.when(z < 8)
    def _():
        for g in range(3):
            signal(mirror(g))

        @pl.loop(0, Z)
        def _(zz):
            signal(dev(x, zz, (y + 4) % Y, (z // 4 + core) % 2))

    switches = switch_ref[...]
    occ = switches[:16].astype(jnp.float32).astype(jnp.bfloat16)
    nslices = occ.shape[1]
    by_slice = (lax.broadcasted_iota(jnp.int32, (nslices, nocc), 1) // (nocc // nslices)
              == lax.broadcasted_iota(jnp.int32, (nslices, nocc), 0)).astype(jnp.float32).astype(jnp.bfloat16)
    occ_mask = jnp.dot(occ, by_slice, preferred_element_type=jnp.float32).astype(jnp.bfloat16)
    screen = switches[16:20, :16].astype(jnp.float32).astype(jnp.bfloat16)
    widen = (lax.broadcasted_iota(jnp.int32, (16, 2048), 1) // BLK
             == lax.broadcasted_iota(jnp.int32, (16, 2048), 0)).astype(jnp.float32).astype(jnp.bfloat16)
    scr_mask = jnp.dot(screen, widen, preferred_element_type=jnp.float32).astype(jnp.bfloat16)

    for q in range(4):
        load_c(q).wait()
        for nb in range(4 * q, 4 * q + 4):
            rows = slice(nb * BLK, (nb + 1) * BLK)
            cv[rows, :] = cv[rows, :] * occ_mask[nb:nb + 1, :]

    def hop(d, slot):
        if slot < 2:
            src = h.at[core, slot, d]
        elif slot < 6:
            src = ring.at[d, slot - 2]
        else:
            target = (y + Y - 1) % Y if d == 0 else (y + 1) % Y
            src = ring.at[d, 4 + target // 4]
        return remote(src, ring.at[d, slot], ring_s.at[d, slot], ring_r.at[d, slot], nexts[d])

    def to_partner(t, d):
        return remote(h.at[core, t, d], h.at[core, t, d], part_s.at[t, d], part_r.at[t, d], partner)

    for t in range(2):
        for p in (2 * t, 2 * t + 1):
            load_t(p).wait()
            tv[p] = tv[p] * scr_mask[p:p + 1, :]
        lhs = tv[2 * t:2 * t + 2].reshape(2 * BLK, tv.shape[2])
        for n in range(nocc // 256):
            cols = slice(n * 256, (n + 1) * 256)
            r = jnp.dot(lhs, cv[:, cols], preferred_element_type=jnp.float32).astype(jnp.bfloat16)
            h[core, t, 0, :, cols] = r[:BLK]
            h[core, t, 1, :, cols] = r[BLK:]
        if t == 0:
            pl.semaphore_wait(barrier, 31 - 3 * (z // 8))
        for d in range(2):
            hop(d, t).start()
        for d in range(2):
            to_partner(t, d).start()

    def dot_nt(a, b):
        return lax.dot_general(a, b, NT, preferred_element_type=jnp.float32)

    for t in range(2):
        for d in range(2):
            to_partner(t, d).wait_recv()
    def chip_rows(t, d):
        return h[:, t, d].reshape(2 * BLK, nocc)

    total = None
    for t in range(2):
        for d in range(2):
            v = dot_nt(chip_rows(t, d), h[core, t, d])
            total = v if total is None else total + v
    blk[0][0, 2] = total[:BLK]
    blk[0][1, 2] = total[BLK:]

    def pair(t, d, slot, rows_own):
        a, b = chip_rows(t, d), ring[d, slot]
        if rows_own:
            r = dot_nt(a, b)
            return r[:BLK], r[BLK:]
        r = dot_nt(b, a)
        return r[:, :BLK], r[:, BLK:]

    def ring_step(s, t):
        slot = 2 * (s - 1) + t
        for d in range(2):
            hop(d, slot).wait_recv()
            if slot < 4:
                hop(d, slot + 2).start()
            elif slot == 5:
                hop(d, 6).start()
        for d in range(2):
            parts = pair(t, d, slot, d == 0)
            for who in range(2):
                if t == 0:
                    blk[s - 1][who, d] = parts[who]
                else:
                    blk[s - 1][who, d] += parts[who]

    def antipode():
        for d in range(2):
            hop(d, 6).wait_recv()

        for side in range(2):
            @pl.when(high == side)
            def _():
                left = pair(side, 0, 6, side == 0)
                right = pair(side, 1, 6, side == 0)
                for who in range(2):
                    blk[3][who, 0] = left[who] + right[who]

    def wait_bytes(ref, sem):
        pltpu.make_async_copy(ref, ref, sem).wait()

    def quarter(xx):
        return pl.ds(pl.multiple_of(xx * QUART, QUART), QUART)

    def when_owner(g, fn):
        if OWNERS[g] == Z:
            fn()
        else:
            pl.when(z < OWNERS[g])(fn)

    def when_mirrored(fn):
        pl.when(z < 8)(fn)

    def xrs_start(g):
        for d in range(X):
            q = quarter((x + d) % X)
            if d:
                remote(blk[g].at[core, :, q, :], xa[g].at[d - 1], xs_s.at[g], xs_r.at[g], x_peer(d, core)).start()
            remote(blk[g].at[other, :, q, :], xb[g].at[d], xt_s.at[g], xt_r.at[g], x_peer(d, other)).start()

    def tile(ref, g, zz, first=0):
        sign, k, row = tile_of(g, zz)
        return ref.at[k, sign, pl.ds(pl.multiple_of(first + row, TILE[g]), TILE[g]), :]

    def zrs_start(g):
        wait_bytes(xa[g], xs_r.at[g])
        wait_bytes(xb[g], xt_r.at[g])
        xs[g][core] = (blk[g][core, :, quarter(x), :] + xa[g][0]) + (xa[g][1] + xa[g][2])
        xs[g][other] = (xb[g][0] + xb[g][1]) + (xb[g][2] + xb[g][3])

        if g == 3:
            @pl.loop(0, OWNERS[g])
            def _(zz):
                remote(tile(xs[g], g, zz), zr[g].at[Z - 1 + z], zs_s.at[g], zs_r.at[g],
                       dev(x, zz, (y + 4) % Y, (zz // 4 + core) % 2)).start()

        @pl.loop(1, Z)
        def _(d):
            zz = (z + d) % Z

            def send():
                remote(tile(xs[g], g, zz), zr[g].at[d - 1], zs_s.at[g], zs_r.at[g], z_peer(d)).start()

            if OWNERS[g] == Z:
                send()
            else:
                pl.when(zz < OWNERS[g])(send)

    def exchange(g):
        return remote(zt[g], ze[g], e_s.at[g], e_r.at[g], mirror(g))

    def ex_start(g):
        def collect():
            wait_bytes(zr[g], zs_r.at[g])
            total = tile(xs[g], g, z)[...]
            for d in range(SOURCES[g]):
                total = total + zr[g][d]
            zt[g][...] = total

        when_owner(g, collect)
        if g < 3:
            when_mirrored(lambda: exchange(g).start())

    def zag_start(g):
        @pl.when(z < 8)
        def _():
            total = zt[g][...]
            if g < 3:
                exchange(g).wait_recv()
                total = total + ze[g][...]
            tile(full[g], g, z, x * QUART)[...] = total

        if g == 0:
            @pl.when(z >= 8)
            def _():
                tile(full[g], g, z, x * QUART)[...] = zt[g][...]

        def spread_out():
            @pl.loop(1, Z)
            def _(d):
                mine = tile(full[g], g, z, x * QUART)
                remote(mine, mine, zg_s.at[g], zg_r.at[g], z_peer(d)).start()

        when_owner(g, spread_out)

    def x_slab(g):
        return full[g].at[:, :, quarter(x), :]

    def three_quarters(g):
        return full[g].at[:, :, pl.ds(0, 3 * QUART), :]

    def xag_start(g):
        if OWNERS[g] == Z:
            wait_bytes(zr[g], zg_r.at[g])
        else:
            @pl.when(z < OWNERS[g])
            def _():
                wait_bytes(zr[g].at[pl.ds(0, OWNERS[g] - 1)], zg_r.at[g])

            @pl.when(z >= OWNERS[g])
            def _():
                wait_bytes(zr[g].at[pl.ds(0, OWNERS[g])], zg_r.at[g])
        for d in range(1, X):
            remote(x_slab(g), x_slab(g), xg_s.at[g], xg_r.at[g], x_peer(d, core)).start()

    def put(d, k, value):
        out_ref[:, pl.ds(pl.multiple_of((2 * d + k) * BLK, BLK), BLK)] = value

    def finish(g):
        wait_bytes(three_quarters(g), xg_r.at[g])
        s = g + 1
        if g < 3:
            for k in range(2):
                put((y + s) % Y, k, full[g][k, 0])
                put((y + Y - s) % Y, k, full[g][k, 1].T)
                if g == 0:
                    put(y, k, full[g][k, 2])
        else:
            for side in range(2):
                @pl.when(high == side)
                def _():
                    for k in range(2):
                        v = full[g][k, 0]
                        put((y + 4) % Y, k, v if side == 0 else v.T)

    ring_step(1, 0)
    ring_step(1, 1)
    xrs_start(0)
    ring_step(2, 0)
    zrs_start(0)
    ring_step(2, 1)
    xrs_start(1)
    ring_step(3, 0)
    ex_start(0)
    zrs_start(1)
    ring_step(3, 1)
    xrs_start(2)
    zag_start(0)
    antipode()
    xrs_start(3)
    ex_start(1)
    zrs_start(2)
    xag_start(0)
    zag_start(1)
    zrs_start(3)
    ex_start(2)
    xag_start(1)
    zag_start(2)
    ex_start(3)
    finish(0)
    zag_start(3)
    finish(1)
    xag_start(2)
    xag_start(3)

    for t in range(2):
        for d in range(2):
            to_partner(t, d).wait_send()
    for d in range(2):
        for slot in range(7):
            hop(d, slot).wait_send()
    for g in range(GROUPS):
        wait_bytes(xa[g], xs_s.at[g])
        wait_bytes(xb[g], xt_s.at[g])
        spread = zr[g].at[pl.ds(0, Z - 1)]
        if OWNERS[g] == Z:
            wait_bytes(spread, zs_s.at[g])
            wait_bytes(spread, zg_s.at[g])
        else:
            sent = OWNERS[g] * (2 if g == 3 else 1)

            @pl.when(z < OWNERS[g])
            def _():
                wait_bytes(zr[g].at[pl.ds(0, sent - 1)], zs_s.at[g])
                wait_bytes(spread, zg_s.at[g])

            @pl.when(z >= OWNERS[g])
            def _():
                wait_bytes(zr[g].at[pl.ds(0, sent)], zs_s.at[g])
        if g < 3:
            when_mirrored(lambda: exchange(g).wait_send())
    finish(2)
    finish(3)
    for g in range(GROUPS):
        wait_bytes(three_quarters(g), xg_s.at[g])


def on_device(three_centre, screening, coefficients, occ_pattern):
    nocc = coefficients.shape[1]
    norb = coefficients.shape[0]
    bf, f32 = jnp.bfloat16, jnp.float32
    dma = pltpu.SemaphoreType.DMA
    vmem = pltpu.VMEM
    nslices = occ_pattern.shape[1]
    switches = jnp.concatenate(
        [occ_pattern, jnp.pad(screening[:, 0, :], ((0, 4), (0, nslices - screening.shape[2])))], axis=0)
    return pl.pallas_call(
        kernel,
        out_shape=jax.ShapeDtypeStruct((BLK, norb), f32),
        in_specs=[pl.BlockSpec(memory_space=pl.ANY)] * 2 + [pl.BlockSpec(memory_space=vmem)],
        out_specs=pl.BlockSpec(memory_space=vmem),
        scratch_shapes=[
            vmem((4, BLK, norb), bf),
            vmem((norb, nocc), bf),
            vmem((2, 2, 2, BLK, nocc), bf),
            vmem((2, 7, BLK, nocc), bf),
            *[vmem((2, n, BLK, BLK), f32) for n in SIGNS],
            *[vmem((X - 1, n, QUART, BLK), f32) for n in SIGNS],
            *[vmem((X, n, QUART, BLK), f32) for n in SIGNS],
            *[vmem((2, n, QUART, BLK), f32) for n in SIGNS],
            *[vmem((n, r, BLK), f32) for n, r in zip(SOURCES, TILE)],
            *[vmem((r, BLK), f32) for r in TILE],
            *[vmem((r, BLK), f32) for r in TILE[:3]],
            *[vmem((2, n, BLK, BLK), f32) for n in SIGNS],
            dma((8,)),
            dma((2, 2)), dma((2, 2)),
            dma((2, 7)), dma((2, 7)),
            *[dma((GROUPS,))] * 12,
        ],
        compiler_params=pltpu.CompilerParams(
            collective_id=0, has_side_effects=True, vmem_limit_bytes=52 * 2**20),
        cost_estimate=pl.CostEstimate(flops=3 * 10**9, bytes_accessed=6 * 10**6, transcendentals=0),
    )(three_centre, coefficients, switches)


def solution(mesh):
    return jax.shard_map(
        on_device,
        mesh=mesh,
        in_specs=(P("aux", "orb", None), P("aux", "orb", None), P(), P()),
        out_specs=P("orb", None),
        check_vma=False,
    )
```

```python
import jax
import jax.numpy as jnp
from jax import lax
from jax.experimental import pallas as pl
from jax.experimental.pallas import tpu as pltpu
from jax.sharding import PartitionSpec as P

MESH = pl.DeviceIdType.MESH
X, Y, Z = 4, 8, 12
BLK = 128
NT = (((1,), (1,)), ((), ()))


SIGNS = (3, 2, 2, 1)
TILE = (16, 16, 16, 8)
OWNERS = (12, 8, 8, 8)
GROUPS = len(SIGNS)
QUART = BLK // X


def kernel(t_hbm, c_hbm, switch_ref, out_ref,
           tv, cv, h, ring,
           blk0, blk1, blk2, blk3,
           xa0, xa1, xa2, xa3, xb0, xb1, xb2, xb3, xs0, xs1, xs2, xs3,
           zr0, zr1, zr2, zr3, zt0, zt1, zt2, zt3, ze0, ze1, ze2, ze3,
           full0, full1, full2, full3,
           load_sem, part_s, part_r, ring_s, ring_r,
           xs_s, xs_r, xt_s, xt_r, zs_s, zs_r, e_s, e_r, zg_s, zg_r, xg_s, xg_r):
    blk = (blk0, blk1, blk2, blk3)
    xa, xb, xs = (xa0, xa1, xa2, xa3), (xb0, xb1, xb2, xb3), (xs0, xs1, xs2, xs3)
    zr, zt, ze = (zr0, zr1, zr2, zr3), (zt0, zt1, zt2, zt3), (ze0, ze1, ze2, ze3)
    full = (full0, full1, full2, full3)
    aux = lax.axis_index("aux")
    orb = lax.axis_index("orb")
    x, z = aux // Z, aux % Z
    y, core = orb // 2, orb % 2
    other = 1 - core
    high = y // 4
    nocc = cv.shape[1]

    def dev(xx, zz, yy, cc):
        return (xx * Z + zz, yy * 2 + cc)

    def remote(src, dst, s_sem, r_sem, where):
        return pltpu.make_async_remote_copy(
            src_ref=src, dst_ref=dst, send_sem=s_sem, recv_sem=r_sem,
            device_id=where, device_id_type=MESH)

    partner = dev(x, z, y, other)
    nexts = (dev(x, z, (y + Y - 1) % Y, core), dev(x, z, (y + 1) % Y, core))

    def tile_of(g, zz):
        if g == 3:
            return 0, (zz // 4 + core) % 2, (zz % 4) * TILE[g]
        a, b, part = zz // 4, (zz // 2) % 2, zz % 2
        flip = (a + (y // 2 if g == 1 else y)) % 2
        sign = (1 - a // 2) * flip + (a // 2) * 2 if g == 0 else flip
        return sign, (b + core) % 2, part * TILE[g]

    def mirror(g):
        sign, k, _ = tile_of(g, z)
        dy = 4 if g == 3 else (1 - sign) * (g + 1) + sign * (Y - g - 1)
        return dev(x, z, (y + dy) % Y, k)

    def x_peer(d, cc):
        return dev((x + d) % X, z, y, cc)

    def z_peer(d):
        return dev(x, (z + d) % Z, y, core)

    def load_t(p):
        f, d = p // 2, p % 2
        source = 2 * ((f + 1 + high) % 2) + d
        return pltpu.make_async_copy(t_hbm.at[source], tv.at[p], load_sem.at[p])

    crows = cv.shape[0] // 4

    def load_c(q):
        rows = pl.ds(q * crows, crows)
        return pltpu.make_async_copy(c_hbm.at[rows], cv.at[rows], load_sem.at[4 + q])

    for q in range(4):
        load_c(q).start()
    for p in range(4):
        load_t(p).start()

    barrier = pltpu.get_barrier_semaphore()

    def signal(where):
        pl.semaphore_signal(barrier, inc=1, device_id=where, device_id_type=MESH)

    signal(partner)
    signal(nexts[0])
    signal(nexts[1])
    for d in range(X):
        if d:
            signal(x_peer(d, core))
            signal(x_peer(d, other))

    @pl.loop(1, Z)
    def _(d):
        signal(z_peer(d))

    @pl.when(z < 8)
    def _():
        for g in range(GROUPS):
            signal(mirror(g))

    switches = switch_ref[...]
    occ = switches[:16].astype(jnp.float32).astype(jnp.bfloat16)
    nslices = occ.shape[1]
    spread = (lax.broadcasted_iota(jnp.int32, (nslices, nocc), 1) // (nocc // nslices)
              == lax.broadcasted_iota(jnp.int32, (nslices, nocc), 0)).astype(jnp.float32).astype(jnp.bfloat16)
    occ_mask = jnp.dot(occ, spread, preferred_element_type=jnp.float32).astype(jnp.bfloat16)
    screen = switches[16:20, :16].astype(jnp.float32).astype(jnp.bfloat16)
    widen = (lax.broadcasted_iota(jnp.int32, (16, 2048), 1) // BLK
             == lax.broadcasted_iota(jnp.int32, (16, 2048), 0)).astype(jnp.float32).astype(jnp.bfloat16)
    scr_mask = jnp.dot(screen, widen, preferred_element_type=jnp.float32).astype(jnp.bfloat16)

    for q in range(4):
        load_c(q).wait()
        for nb in range(4 * q, 4 * q + 4):
            rows = slice(nb * BLK, (nb + 1) * BLK)
            cv[rows, :] = cv[rows, :] * occ_mask[nb:nb + 1, :]

    def hop(d, slot):
        if slot < 2:
            src = h.at[core, slot, d]
        elif slot < 6:
            src = ring.at[d, slot - 2]
        else:
            src = ring.at[d, 4]
        return remote(src, ring.at[d, slot], ring_s.at[d, slot], ring_r.at[d, slot], nexts[d])

    def to_partner(t, d):
        return remote(h.at[core, t, d], h.at[core, t, d], part_s.at[t, d], part_r.at[t, d], partner)

    for t in range(2):
        for p in (2 * t, 2 * t + 1):
            load_t(p).wait()
            f, d = p // 2, p % 2
            own_mask = jnp.where(high == 1 - f, scr_mask[d:d + 1, :], scr_mask[2 + d:3 + d, :])
            tv[p] = tv[p] * own_mask
        lhs = tv[2 * t:2 * t + 2].reshape(2 * BLK, tv.shape[2])
        for n in range(nocc // 256):
            cols = slice(n * 256, (n + 1) * 256)
            r = jnp.dot(lhs, cv[:, cols], preferred_element_type=jnp.float32).astype(jnp.bfloat16)
            h[core, t, 0, :, cols] = r[:BLK]
            h[core, t, 1, :, cols] = r[BLK:]
        if t == 0:
            pl.semaphore_wait(barrier, 24 - 4 * (z // 8))
        for d in range(2):
            hop(d, t).start()
        for d in range(2):
            to_partner(t, d).start()

    def dot_nt(a, b):
        return lax.dot_general(a, b, NT, preferred_element_type=jnp.float32)

    for t in range(2):
        for d in range(2):
            to_partner(t, d).wait_recv()
    def chip_rows(t, d):
        return h[:, t, d].reshape(2 * BLK, nocc)

    total = None
    for t in range(2):
        for d in range(2):
            v = dot_nt(chip_rows(t, d), h[core, t, d])
            total = v if total is None else total + v
    blk[0][0, 2] = total[:BLK]
    blk[0][1, 2] = total[BLK:]

    def pair(t, d, slot, rows_own):
        a, b = chip_rows(t, d), ring[d, slot]
        if rows_own:
            r = dot_nt(a, b)
            return r[:BLK], r[BLK:]
        r = dot_nt(b, a)
        return r[:, :BLK], r[:, BLK:]

    def ring_step(s, t):
        slot = 2 * (s - 1) + t
        for d in range(2):
            hop(d, slot).wait_recv()
            if slot < 4:
                hop(d, slot + 2).start()
            elif slot == 4:
                hop(d, 6).start()
        for d in range(2):
            sender = (y + s) % Y if d == 0 else (y + Y - s) % Y
            parts = pair((t + sender // 4 + high) % 2, d, slot, d == 0)
            for who in range(2):
                if t == 0:
                    blk[s - 1][who, d] = parts[who]
                else:
                    blk[s - 1][who, d] += parts[who]

    def antipode():
        for d in range(2):
            hop(d, 6).wait_recv()

        for side in range(2):
            @pl.when(high == side)
            def _():
                left = pair(1, 0, 6, side == 0)
                right = pair(1, 1, 6, side == 0)
                for who in range(2):
                    blk[3][who, 0] = left[who] + right[who]

    def wait_bytes(ref, sem):
        pltpu.make_async_copy(ref, ref, sem).wait()

    def quarter(xx):
        return pl.ds(pl.multiple_of(xx * QUART, QUART), QUART)

    def when_owner(g, fn):
        if OWNERS[g] == Z:
            fn()
        else:
            pl.when(z < OWNERS[g])(fn)

    def when_mirrored(fn):
        pl.when(z < 8)(fn)

    def xrs_start(g):
        for d in range(X):
            q = quarter((x + d) % X)
            if d:
                remote(blk[g].at[core, :, q, :], xa[g].at[d - 1], xs_s.at[g], xs_r.at[g], x_peer(d, core)).start()
            remote(blk[g].at[other, :, q, :], xb[g].at[d], xt_s.at[g], xt_r.at[g], x_peer(d, other)).start()

    def tile(ref, g, zz, first=0):
        sign, k, row = tile_of(g, zz)
        return ref.at[k, sign, pl.ds(pl.multiple_of(first + row, TILE[g]), TILE[g]), :]

    def zrs_start(g):
        wait_bytes(xa[g], xs_r.at[g])
        wait_bytes(xb[g], xt_r.at[g])
        xs[g][core] = (blk[g][core, :, quarter(x), :] + xa[g][0]) + (xa[g][1] + xa[g][2])
        xs[g][other] = (xb[g][0] + xb[g][1]) + (xb[g][2] + xb[g][3])

        @pl.loop(1, Z)
        def _(d):
            zz = (z + d) % Z

            def send():
                remote(tile(xs[g], g, zz), zr[g].at[d - 1], zs_s.at[g], zs_r.at[g], z_peer(d)).start()

            if OWNERS[g] == Z:
                send()
            else:
                pl.when(zz < OWNERS[g])(send)

    def exchange(g):
        return remote(zt[g], ze[g], e_s.at[g], e_r.at[g], mirror(g))

    def ex_start(g):
        def collect():
            wait_bytes(zr[g], zs_r.at[g])
            total = tile(xs[g], g, z)[...]
            for d in range(Z - 1):
                total = total + zr[g][d]
            zt[g][...] = total

        when_owner(g, collect)
        when_mirrored(lambda: exchange(g).start())

    def zag_start(g):
        @pl.when(z < 8)
        def _():
            exchange(g).wait_recv()
            tile(full[g], g, z, x * QUART)[...] = zt[g][...] + ze[g][...]

        if g == 0:
            @pl.when(z >= 8)
            def _():
                tile(full[g], g, z, x * QUART)[...] = zt[g][...]

        def spread_out():
            @pl.loop(1, Z)
            def _(d):
                mine = tile(full[g], g, z, x * QUART)
                remote(mine, mine, zg_s.at[g], zg_r.at[g], z_peer(d)).start()

        when_owner(g, spread_out)

    def x_slab(g):
        return full[g].at[:, :, quarter(x), :]

    def three_quarters(g):
        return full[g].at[:, :, pl.ds(0, 3 * QUART), :]

    def xag_start(g):
        if OWNERS[g] == Z:
            wait_bytes(zr[g], zg_r.at[g])
        else:
            @pl.when(z < OWNERS[g])
            def _():
                wait_bytes(zr[g].at[pl.ds(0, OWNERS[g] - 1)], zg_r.at[g])

            @pl.when(z >= OWNERS[g])
            def _():
                wait_bytes(zr[g].at[pl.ds(0, OWNERS[g])], zg_r.at[g])
        for d in range(1, X):
            remote(x_slab(g), x_slab(g), xg_s.at[g], xg_r.at[g], x_peer(d, core)).start()

    def put(d, k, value):
        out_ref[:, pl.ds(pl.multiple_of((2 * d + k) * BLK, BLK), BLK)] = value

    def finish(g):
        wait_bytes(three_quarters(g), xg_r.at[g])
        s = g + 1
        if g < 3:
            for k in range(2):
                put((y + s) % Y, k, full[g][k, 0])
                put((y + Y - s) % Y, k, full[g][k, 1].T)
                if g == 0:
                    put(y, k, full[g][k, 2])
        else:
            for side in range(2):
                @pl.when(high == side)
                def _():
                    for k in range(2):
                        v = full[g][k, 0]
                        put((y + 4) % Y, k, v if side == 0 else v.T)

    ring_step(1, 0)
    ring_step(1, 1)
    xrs_start(0)
    ring_step(2, 0)
    zrs_start(0)
    ring_step(2, 1)
    xrs_start(1)
    ring_step(3, 0)
    ex_start(0)
    zrs_start(1)
    ring_step(3, 1)
    xrs_start(2)
    zag_start(0)
    antipode()
    xrs_start(3)
    ex_start(1)
    zrs_start(2)
    xag_start(0)
    zag_start(1)
    zrs_start(3)
    ex_start(2)
    xag_start(1)
    zag_start(2)
    ex_start(3)
    finish(0)
    zag_start(3)
    finish(1)
    xag_start(2)
    xag_start(3)
    finish(2)
    finish(3)

    for t in range(2):
        for d in range(2):
            to_partner(t, d).wait_send()
    for d in range(2):
        for slot in range(7):
            hop(d, slot).wait_send()
    for g in range(GROUPS):
        wait_bytes(xa[g], xs_s.at[g])
        wait_bytes(xb[g], xt_s.at[g])
        if OWNERS[g] == Z:
            wait_bytes(zr[g], zs_s.at[g])
            wait_bytes(zr[g], zg_s.at[g])
        else:
            @pl.when(z < OWNERS[g])
            def _():
                wait_bytes(zr[g].at[pl.ds(0, OWNERS[g] - 1)], zs_s.at[g])
                wait_bytes(zr[g], zg_s.at[g])

            @pl.when(z >= OWNERS[g])
            def _():
                wait_bytes(zr[g].at[pl.ds(0, OWNERS[g])], zs_s.at[g])
        when_mirrored(lambda: exchange(g).wait_send())
        wait_bytes(three_quarters(g), xg_s.at[g])


def on_device(three_centre, screening, coefficients, occ_pattern):
    nocc = coefficients.shape[1]
    norb = coefficients.shape[0]
    bf, f32 = jnp.bfloat16, jnp.float32
    dma = pltpu.SemaphoreType.DMA
    vmem = pltpu.VMEM
    nslices = occ_pattern.shape[1]
    switches = jnp.concatenate(
        [occ_pattern, jnp.pad(screening[:, 0, :], ((0, 4), (0, nslices - screening.shape[2])))], axis=0)
    return pl.pallas_call(
        kernel,
        out_shape=jax.ShapeDtypeStruct((BLK, norb), f32),
        in_specs=[pl.BlockSpec(memory_space=pl.ANY)] * 2 + [pl.BlockSpec(memory_space=vmem)],
        out_specs=pl.BlockSpec(memory_space=vmem),
        scratch_shapes=[
            vmem((4, BLK, norb), bf),
            vmem((norb, nocc), bf),
            vmem((2, 2, 2, BLK, nocc), bf),
            vmem((2, 7, BLK, nocc), bf),
            *[vmem((2, n, BLK, BLK), f32) for n in SIGNS],
            *[vmem((X - 1, n, QUART, BLK), f32) for n in SIGNS],
            *[vmem((X, n, QUART, BLK), f32) for n in SIGNS],
            *[vmem((2, n, QUART, BLK), f32) for n in SIGNS],
            *[vmem((Z - 1, r, BLK), f32) for r in TILE],
            *[vmem((r, BLK), f32) for r in TILE],
            *[vmem((r, BLK), f32) for r in TILE],
            *[vmem((2, n, BLK, BLK), f32) for n in SIGNS],
            dma((8,)),
            dma((2, 2)), dma((2, 2)),
            dma((2, 7)), dma((2, 7)),
            *[dma((GROUPS,))] * 12,
        ],
        compiler_params=pltpu.CompilerParams(
            collective_id=0, has_side_effects=True, vmem_limit_bytes=52 * 2**20),
        cost_estimate=pl.CostEstimate(flops=3 * 10**9, bytes_accessed=6 * 10**6, transcendentals=0),
    )(three_centre, coefficients, switches)


def solution(mesh):
    return jax.shard_map(
        on_device,
        mesh=mesh,
        in_specs=(P("aux", "orb", None), P("aux", "orb", None), P(), P()),
        out_specs=P("orb", None),
        check_vma=False,
    )
```

```python
import jax
import jax.numpy as jnp
from jax import lax
from jax.experimental import pallas as pl
from jax.experimental.pallas import tpu as pltpu
from jax.sharding import PartitionSpec as P

MESH = pl.DeviceIdType.MESH
X, Y, Z = 4, 8, 12
BLK = 128
NT = (((1,), (1,)), ((), ()))


SIGNS = (3, 2, 2, 1)
TILE = (16, 16, 16, 8)
OWNERS = (12, 8, 8, 8)
GROUPS = len(SIGNS)
QUART = BLK // X


def kernel(t_hbm, c_hbm, switch_ref, out_ref,
           tv, cv, h, ring,
           blk0, blk1, blk2, blk3,
           xa0, xa1, xa2, xa3, xb0, xb1, xb2, xb3, xs0, xs1, xs2, xs3,
           zr0, zr1, zr2, zr3, zt0, zt1, zt2, zt3, ze0, ze1, ze2, ze3,
           full0, full1, full2, full3,
           load_sem, part_s, part_r, ring_s, ring_r,
           xs_s, xs_r, xt_s, xt_r, zs_s, zs_r, e_s, e_r, zg_s, zg_r, xg_s, xg_r, known):
    blk = (blk0, blk1, blk2, blk3)
    xa, xb, xs = (xa0, xa1, xa2, xa3), (xb0, xb1, xb2, xb3), (xs0, xs1, xs2, xs3)
    zr, zt, ze = (zr0, zr1, zr2, zr3), (zt0, zt1, zt2, zt3), (ze0, ze1, ze2, ze3)
    full = (full0, full1, full2, full3)
    aux = lax.axis_index("aux")
    orb = lax.axis_index("orb")
    x, z = aux // Z, aux % Z
    y, core = orb // 2, orb % 2
    other = 1 - core
    high = y // 4
    nocc = cv.shape[1]

    def dev(xx, zz, yy, cc):
        return (xx * Z + zz, yy * 2 + cc)

    def remote(src, dst, s_sem, r_sem, where):
        return pltpu.make_async_remote_copy(
            src_ref=src, dst_ref=dst, send_sem=s_sem, recv_sem=r_sem,
            device_id=where, device_id_type=MESH)

    partner = dev(x, z, y, other)
    nexts = (dev(x, z, (y + Y - 1) % Y, core), dev(x, z, (y + 1) % Y, core))

    def tile_of(g, zz):
        if g == 3:
            return 0, (zz // 4 + core) % 2, (zz % 4) * TILE[g]
        a, b, part = zz // 4, (zz // 2) % 2, zz % 2
        flip = (a + (y // 2 if g == 1 else y)) % 2
        sign = (1 - a // 2) * flip + (a // 2) * 2 if g == 0 else flip
        return sign, (b + core) % 2, part * TILE[g]

    def mirror(g):
        sign, k, _ = tile_of(g, z)
        dy = 4 if g == 3 else (1 - sign) * (g + 1) + sign * (Y - g - 1)
        return dev(x, z, (y + dy) % Y, k)

    def x_peer(d, cc):
        return dev((x + d) % X, z, y, cc)

    def z_peer(d):
        return dev(x, (z + d) % Z, y, core)

    def load_t(p):
        f, d = p // 2, p % 2
        source = 2 * ((f + 1 + high) % 2) + d
        return pltpu.make_async_copy(t_hbm.at[source], tv.at[p], load_sem.at[p])

    crows = cv.shape[0] // 4

    def load_c(q):
        rows = pl.ds(q * crows, crows)
        return pltpu.make_async_copy(c_hbm.at[rows], cv.at[rows], load_sem.at[4 + q])

    for q in range(4):
        load_c(q).start()
    for p in range(4):
        load_t(p).start()

    barrier = pltpu.get_barrier_semaphore()

    def signal(where):
        pl.semaphore_signal(barrier, inc=1, device_id=where, device_id_type=MESH)

    signal(partner)
    signal(nexts[0])
    signal(nexts[1])
    for d in range(X):
        if d:
            signal(x_peer(d, core))
            signal(x_peer(d, other))

    signal(z_peer(1))
    signal(z_peer(Z - 1))

    def tell(r):
        for d in (2 ** r, Z - 2 ** r):
            pl.semaphore_signal(known.at[r], inc=1, device_id=z_peer(d), device_id_type=MESH)

    def hear(r):
        pl.semaphore_wait(known.at[r], 2)

    switches = switch_ref[...]
    occ = switches[:16].astype(jnp.float32).astype(jnp.bfloat16)
    nslices = occ.shape[1]
    spread = (lax.broadcasted_iota(jnp.int32, (nslices, nocc), 1) // (nocc // nslices)
              == lax.broadcasted_iota(jnp.int32, (nslices, nocc), 0)).astype(jnp.float32).astype(jnp.bfloat16)
    occ_mask = jnp.dot(occ, spread, preferred_element_type=jnp.float32).astype(jnp.bfloat16)
    screen = switches[16:20, :16].astype(jnp.float32).astype(jnp.bfloat16)
    widen = (lax.broadcasted_iota(jnp.int32, (16, 2048), 1) // BLK
             == lax.broadcasted_iota(jnp.int32, (16, 2048), 0)).astype(jnp.float32).astype(jnp.bfloat16)
    scr_mask = jnp.dot(screen, widen, preferred_element_type=jnp.float32).astype(jnp.bfloat16)

    for q in range(4):
        load_c(q).wait()
        for nb in range(4 * q, 4 * q + 4):
            rows = slice(nb * BLK, (nb + 1) * BLK)
            cv[rows, :] = cv[rows, :] * occ_mask[nb:nb + 1, :]

    def hop(d, slot):
        if slot < 2:
            src = h.at[core, slot, d]
        elif slot < 6:
            src = ring.at[d, slot - 2]
        else:
            src = ring.at[d, 4]
        return remote(src, ring.at[d, slot], ring_s.at[d, slot], ring_r.at[d, slot], nexts[d])

    def to_partner(t, d):
        return remote(h.at[core, t, d], h.at[core, t, d], part_s.at[t, d], part_r.at[t, d], partner)

    for t in range(2):
        for p in (2 * t, 2 * t + 1):
            load_t(p).wait()
            f, d = p // 2, p % 2
            own_mask = jnp.where(high == 1 - f, scr_mask[d:d + 1, :], scr_mask[2 + d:3 + d, :])
            tv[p] = tv[p] * own_mask
        lhs = tv[2 * t:2 * t + 2].reshape(2 * BLK, tv.shape[2])
        for n in range(nocc // 256):
            cols = slice(n * 256, (n + 1) * 256)
            r = jnp.dot(lhs, cv[:, cols], preferred_element_type=jnp.float32).astype(jnp.bfloat16)
            h[core, t, 0, :, cols] = r[:BLK]
            h[core, t, 1, :, cols] = r[BLK:]
        if t == 0:
            pl.semaphore_wait(barrier, 11)
        for d in range(2):
            hop(d, t).start()
        for d in range(2):
            to_partner(t, d).start()

    def dot_nt(a, b):
        return lax.dot_general(a, b, NT, preferred_element_type=jnp.float32)

    for t in range(2):
        for d in range(2):
            to_partner(t, d).wait_recv()
    def chip_rows(t, d):
        return h[:, t, d].reshape(2 * BLK, nocc)

    total = None
    for t in range(2):
        for d in range(2):
            v = dot_nt(chip_rows(t, d), h[core, t, d])
            total = v if total is None else total + v
    blk[0][0, 2] = total[:BLK]
    blk[0][1, 2] = total[BLK:]

    def pair(t, d, slot, rows_own):
        a, b = chip_rows(t, d), ring[d, slot]
        if rows_own:
            r = dot_nt(a, b)
            return r[:BLK], r[BLK:]
        r = dot_nt(b, a)
        return r[:, :BLK], r[:, BLK:]

    def ring_step(s, t):
        slot = 2 * (s - 1) + t
        for d in range(2):
            hop(d, slot).wait_recv()
            if slot < 4:
                hop(d, slot + 2).start()
        for d in range(2):
            sender = (y + s) % Y if d == 0 else (y + Y - s) % Y
            parts = pair((t + sender // 4 + high) % 2, d, slot, d == 0)
            for who in range(2):
                if t == 0:
                    blk[s - 1][who, d] = parts[who]
                else:
                    blk[s - 1][who, d] += parts[who]

    def last_hop():
        for d in range(2):
            hop(d, 5).wait_send()
            hop(d, 6).start()

    def antipode():
        for d in range(2):
            hop(d, 6).wait_recv()

        for side in range(2):
            @pl.when(high == side)
            def _():
                left = pair(1, 0, 6, side == 0)
                right = pair(1, 1, 6, side == 0)
                for who in range(2):
                    blk[3][who, 0] = left[who] + right[who]

    def wait_bytes(ref, sem):
        pltpu.make_async_copy(ref, ref, sem).wait()

    def quarter(xx):
        return pl.ds(pl.multiple_of(xx * QUART, QUART), QUART)

    def when_owner(g, fn):
        if OWNERS[g] == Z:
            fn()
        else:
            pl.when(z < OWNERS[g])(fn)

    def when_mirrored(fn):
        pl.when(z < 8)(fn)

    def xrs_start(g):
        for d in range(X):
            q = quarter((x + d) % X)
            if d:
                remote(blk[g].at[core, :, q, :], xa[g].at[d - 1], xs_s.at[g], xs_r.at[g], x_peer(d, core)).start()
            remote(blk[g].at[other, :, q, :], xb[g].at[d], xt_s.at[g], xt_r.at[g], x_peer(d, other)).start()

    def tile(ref, g, zz, first=0):
        sign, k, row = tile_of(g, zz)
        return ref.at[k, sign, pl.ds(pl.multiple_of(first + row, TILE[g]), TILE[g]), :]

    def zrs_start(g):
        wait_bytes(xa[g], xs_r.at[g])
        wait_bytes(xb[g], xt_r.at[g])
        xs[g][core] = (blk[g][core, :, quarter(x), :] + xa[g][0]) + (xa[g][1] + xa[g][2])
        xs[g][other] = (xb[g][0] + xb[g][1]) + (xb[g][2] + xb[g][3])

        @pl.loop(1, Z)
        def _(d):
            zz = (z + d) % Z

            def send():
                remote(tile(xs[g], g, zz), zr[g].at[d - 1], zs_s.at[g], zs_r.at[g], z_peer(d)).start()

            if OWNERS[g] == Z:
                send()
            else:
                pl.when(zz < OWNERS[g])(send)

    def exchange(g):
        return remote(zt[g], ze[g], e_s.at[g], e_r.at[g], mirror(g))

    def ex_start(g):
        def collect():
            wait_bytes(zr[g], zs_r.at[g])
            total = tile(xs[g], g, z)[...]
            for d in range(Z - 1):
                total = total + zr[g][d]
            zt[g][...] = total

        when_owner(g, collect)
        when_mirrored(lambda: exchange(g).start())

    def zag_start(g):
        @pl.when(z < 8)
        def _():
            exchange(g).wait_recv()
            tile(full[g], g, z, x * QUART)[...] = zt[g][...] + ze[g][...]

        if g == 0:
            @pl.when(z >= 8)
            def _():
                tile(full[g], g, z, x * QUART)[...] = zt[g][...]

        def spread_out():
            @pl.loop(1, Z)
            def _(d):
                mine = tile(full[g], g, z, x * QUART)
                remote(mine, mine, zg_s.at[g], zg_r.at[g], z_peer(d)).start()

        when_owner(g, spread_out)

    def x_slab(g):
        return full[g].at[:, :, quarter(x), :]

    def three_quarters(g):
        return full[g].at[:, :, pl.ds(0, 3 * QUART), :]

    def xag_start(g):
        if OWNERS[g] == Z:
            wait_bytes(zr[g], zg_r.at[g])
        else:
            @pl.when(z < OWNERS[g])
            def _():
                wait_bytes(zr[g].at[pl.ds(0, OWNERS[g] - 1)], zg_r.at[g])

            @pl.when(z >= OWNERS[g])
            def _():
                wait_bytes(zr[g].at[pl.ds(0, OWNERS[g])], zg_r.at[g])
        for d in range(1, X):
            remote(x_slab(g), x_slab(g), xg_s.at[g], xg_r.at[g], x_peer(d, core)).start()

    def put(d, k, value):
        out_ref[:, pl.ds(pl.multiple_of((2 * d + k) * BLK, BLK), BLK)] = value

    def finish(g):
        wait_bytes(three_quarters(g), xg_r.at[g])
        s = g + 1
        if g < 3:
            for k in range(2):
                put((y + s) % Y, k, full[g][k, 0])
                put((y + Y - s) % Y, k, full[g][k, 1].T)
                if g == 0:
                    put(y, k, full[g][k, 2])
        else:
            for side in range(2):
                @pl.when(high == side)
                def _():
                    for k in range(2):
                        v = full[g][k, 0]
                        put((y + 4) % Y, k, v if side == 0 else v.T)

    tell(0)
    hear(0)
    tell(1)
    ring_step(1, 0)
    hear(1)
    tell(2)
    ring_step(1, 1)
    xrs_start(0)
    ring_step(2, 0)
    hear(2)
    zrs_start(0)
    ring_step(2, 1)
    xrs_start(1)
    ring_step(3, 0)
    ex_start(0)
    zrs_start(1)
    last_hop()
    ring_step(3, 1)
    xrs_start(2)
    zag_start(0)
    antipode()
    xrs_start(3)
    ex_start(1)
    zrs_start(2)
    xag_start(0)
    zag_start(1)
    zrs_start(3)
    ex_start(2)
    xag_start(1)
    zag_start(2)
    ex_start(3)
    finish(0)
    zag_start(3)
    finish(1)
    xag_start(2)
    xag_start(3)
    finish(2)
    finish(3)

    for t in range(2):
        for d in range(2):
            to_partner(t, d).wait_send()
    for d in range(2):
        for slot in (0, 1, 2, 3, 4, 6):
            hop(d, slot).wait_send()
    for g in range(GROUPS):
        wait_bytes(xa[g], xs_s.at[g])
        wait_bytes(xb[g], xt_s.at[g])
        if OWNERS[g] == Z:
            wait_bytes(zr[g], zs_s.at[g])
            wait_bytes(zr[g], zg_s.at[g])
        else:
            @pl.when(z < OWNERS[g])
            def _():
                wait_bytes(zr[g].at[pl.ds(0, OWNERS[g] - 1)], zs_s.at[g])
                wait_bytes(zr[g], zg_s.at[g])

            @pl.when(z >= OWNERS[g])
            def _():
                wait_bytes(zr[g].at[pl.ds(0, OWNERS[g])], zs_s.at[g])
        when_mirrored(lambda: exchange(g).wait_send())
        wait_bytes(three_quarters(g), xg_s.at[g])


def on_device(three_centre, screening, coefficients, occ_pattern):
    nocc = coefficients.shape[1]
    norb = coefficients.shape[0]
    bf, f32 = jnp.bfloat16, jnp.float32
    dma = pltpu.SemaphoreType.DMA
    vmem = pltpu.VMEM
    nslices = occ_pattern.shape[1]
    switches = jnp.concatenate(
        [occ_pattern, jnp.pad(screening[:, 0, :], ((0, 4), (0, nslices - screening.shape[2])))], axis=0)
    return pl.pallas_call(
        kernel,
        out_shape=jax.ShapeDtypeStruct((BLK, norb), f32),
        in_specs=[pl.BlockSpec(memory_space=pl.ANY)] * 2 + [pl.BlockSpec(memory_space=vmem)],
        out_specs=pl.BlockSpec(memory_space=vmem),
        scratch_shapes=[
            vmem((4, BLK, norb), bf),
            vmem((norb, nocc), bf),
            vmem((2, 2, 2, BLK, nocc), bf),
            vmem((2, 7, BLK, nocc), bf),
            *[vmem((2, n, BLK, BLK), f32) for n in SIGNS],
            *[vmem((X - 1, n, QUART, BLK), f32) for n in SIGNS],
            *[vmem((X, n, QUART, BLK), f32) for n in SIGNS],
            *[vmem((2, n, QUART, BLK), f32) for n in SIGNS],
            *[vmem((Z - 1, r, BLK), f32) for r in TILE],
            *[vmem((r, BLK), f32) for r in TILE],
            *[vmem((r, BLK), f32) for r in TILE],
            *[vmem((2, n, BLK, BLK), f32) for n in SIGNS],
            dma((8,)),
            dma((2, 2)), dma((2, 2)),
            dma((2, 7)), dma((2, 7)),
            *[dma((GROUPS,))] * 12,
            pltpu.SemaphoreType.REGULAR((3,)),
        ],
        compiler_params=pltpu.CompilerParams(
            collective_id=0, has_side_effects=True, vmem_limit_bytes=52 * 2**20),
        cost_estimate=pl.CostEstimate(flops=3 * 10**9, bytes_accessed=6 * 10**6, transcendentals=0),
    )(three_centre, coefficients, switches)


def solution(mesh):
    return jax.shard_map(
        on_device,
        mesh=mesh,
        in_specs=(P("aux", "orb", None), P("aux", "orb", None), P(), P()),
        out_specs=P("orb", None),
        check_vma=False,
    )
```

```python
import jax
import jax.numpy as jnp
from jax import lax
from jax.experimental import pallas as pl
from jax.experimental.pallas import tpu as pltpu
from jax.sharding import PartitionSpec as P

MESH = pl.DeviceIdType.MESH
X, Y, Z = 4, 8, 12
BLK = 128
NT = (((1,), (1,)), ((), ()))


SIGNS = (3, 2, 2, 1)
TILE = (16, 16, 16, 8)
OWNERS = (12, 8, 8, 8)
GROUPS = len(SIGNS)
QUART = BLK // X


def kernel(t_hbm, c_hbm, switch_ref, out_ref,
           tv, cv, h, ring,
           blk0, blk1, blk2, blk3,
           xa0, xa1, xa2, xa3, xb0, xb1, xb2, xb3, xs0, xs1, xs2, xs3,
           zr0, zr1, zr2, zr3, zt0, zt1, zt2, zt3, ze0, ze1, ze2, ze3,
           full0, full1, full2, full3,
           load_sem, part_s, part_r, ring_s, ring_r,
           xs_s, xs_r, xt_s, xt_r, zs_s, zs_r, e_s, e_r, zg_s, zg_r, xg_s, xg_r, known):
    blk = (blk0, blk1, blk2, blk3)
    xa, xb, xs = (xa0, xa1, xa2, xa3), (xb0, xb1, xb2, xb3), (xs0, xs1, xs2, xs3)
    zr, zt, ze = (zr0, zr1, zr2, zr3), (zt0, zt1, zt2, zt3), (ze0, ze1, ze2, ze3)
    full = (full0, full1, full2, full3)
    aux = lax.axis_index("aux")
    orb = lax.axis_index("orb")
    x, z = aux // Z, aux % Z
    y, core = orb // 2, orb % 2
    other = 1 - core
    high = y // 4
    nocc = cv.shape[1]

    def dev(xx, zz, yy, cc):
        return (xx * Z + zz, yy * 2 + cc)

    def remote(src, dst, s_sem, r_sem, where):
        return pltpu.make_async_remote_copy(
            src_ref=src, dst_ref=dst, send_sem=s_sem, recv_sem=r_sem,
            device_id=where, device_id_type=MESH)

    partner = dev(x, z, y, other)
    nexts = (dev(x, z, (y + Y - 1) % Y, core), dev(x, z, (y + 1) % Y, core))

    def tile_of(g, zz):
        if g == 3:
            return 0, (zz // 4 + core) % 2, (zz % 4) * TILE[g]
        a, b, part = zz // 4, (zz // 2) % 2, zz % 2
        flip = (a + (y // 2 if g == 1 else y)) % 2
        sign = (1 - a // 2) * flip + (a // 2) * 2 if g == 0 else flip
        return sign, (b + core) % 2, part * TILE[g]

    def mirror(g):
        sign, k, _ = tile_of(g, z)
        dy = 4 if g == 3 else (1 - sign) * (g + 1) + sign * (Y - g - 1)
        return dev(x, z, (y + dy) % Y, k)

    def x_peer(d, cc):
        return dev((x + d) % X, z, y, cc)

    def z_peer(d):
        return dev(x, (z + d) % Z, y, core)

    def load_t(p):
        f, d = p // 2, p % 2
        source = 2 * ((f + 1 + high) % 2) + d
        return pltpu.make_async_copy(t_hbm.at[source], tv.at[p], load_sem.at[p])

    crows = cv.shape[0] // 4

    def load_c(q):
        rows = pl.ds(q * crows, crows)
        return pltpu.make_async_copy(c_hbm.at[rows], cv.at[rows], load_sem.at[4 + q])

    for q in range(4):
        load_c(q).start()
    for p in range(4):
        load_t(p).start()

    barrier = pltpu.get_barrier_semaphore()

    def signal(where):
        pl.semaphore_signal(barrier, inc=1, device_id=where, device_id_type=MESH)

    signal(partner)
    signal(nexts[0])
    signal(nexts[1])
    for d in range(X):
        if d:
            signal(x_peer(d, core))
            signal(x_peer(d, other))

    signal(z_peer(1))
    signal(z_peer(Z - 1))

    def tell(r):
        for d in (2 ** r, Z - 2 ** r):
            pl.semaphore_signal(known.at[r], inc=1, device_id=z_peer(d), device_id_type=MESH)

    def hear(r):
        pl.semaphore_wait(known.at[r], 2)

    switches = switch_ref[...]
    occ = switches[:16].astype(jnp.float32).astype(jnp.bfloat16)
    nslices = occ.shape[1]
    spread = (lax.broadcasted_iota(jnp.int32, (nslices, nocc), 1) // (nocc // nslices)
              == lax.broadcasted_iota(jnp.int32, (nslices, nocc), 0)).astype(jnp.float32).astype(jnp.bfloat16)
    occ_mask = jnp.dot(occ, spread, preferred_element_type=jnp.float32).astype(jnp.bfloat16)
    screen = switches[16:20, :16].astype(jnp.float32).astype(jnp.bfloat16)
    widen = (lax.broadcasted_iota(jnp.int32, (16, 2048), 1) // BLK
             == lax.broadcasted_iota(jnp.int32, (16, 2048), 0)).astype(jnp.float32).astype(jnp.bfloat16)
    scr_mask = jnp.dot(screen, widen, preferred_element_type=jnp.float32).astype(jnp.bfloat16)

    for q in range(4):
        load_c(q).wait()
        for nb in range(4 * q, 4 * q + 4):
            rows = slice(nb * BLK, (nb + 1) * BLK)
            cv[rows, :] = cv[rows, :] * occ_mask[nb:nb + 1, :]

    def hop(d, slot):
        if slot < 2:
            src = h.at[core, slot, d]
        elif slot < 6:
            src = ring.at[d, slot - 2]
        else:
            src = ring.at[d, 4]
        return remote(src, ring.at[d, slot], ring_s.at[d, slot], ring_r.at[d, slot], nexts[d])

    def to_partner(t, d):
        return remote(h.at[core, t, d], h.at[core, t, d], part_s.at[t, d], part_r.at[t, d], partner)

    for t in range(2):
        for p in (2 * t, 2 * t + 1):
            load_t(p).wait()
            f, d = p // 2, p % 2
            own_mask = jnp.where(high == 1 - f, scr_mask[d:d + 1, :], scr_mask[2 + d:3 + d, :])
            tv[p] = tv[p] * own_mask
        lhs = tv[2 * t:2 * t + 2].reshape(2 * BLK, tv.shape[2])
        for n in range(nocc // 256):
            cols = pl.ds(n * 256, 256)
            r = jnp.dot(lhs, cv[:, cols], preferred_element_type=jnp.float32).astype(jnp.bfloat16)
            h[core, t, 0, :, cols] = r[:BLK]
            h[core, t, 1, :, cols] = r[BLK:]
            if t == 0:
                if n == 0:
                    pl.semaphore_wait(barrier, 11)
                for d in range(2):
                    remote(h.at[core, t, d, :, cols], ring.at[d, t, :, cols],
                           ring_s.at[d, t], ring_r.at[d, t], nexts[d]).start()
        if t == 1:
            for d in range(2):
                hop(d, t).start()
        for d in range(2):
            to_partner(t, d).start()

    def dot_nt(a, b):
        return lax.dot_general(a, b, NT, preferred_element_type=jnp.float32)

    for t in range(2):
        for d in range(2):
            to_partner(t, d).wait_recv()
    def chip_rows(t, d):
        return h[:, t, d].reshape(2 * BLK, nocc)

    total = None
    for t in range(2):
        for d in range(2):
            v = dot_nt(chip_rows(t, d), h[core, t, d])
            total = v if total is None else total + v
    blk[0][0, 2] = total[:BLK]
    blk[0][1, 2] = total[BLK:]

    def pair(t, d, slot, rows_own):
        a, b = chip_rows(t, d), ring[d, slot]
        if rows_own:
            r = dot_nt(a, b)
            return r[:BLK], r[BLK:]
        r = dot_nt(b, a)
        return r[:, :BLK], r[:, BLK:]

    def ring_step(s, t):
        slot = 2 * (s - 1) + t
        for d in range(2):
            hop(d, slot).wait_recv()
            if slot < 4:
                hop(d, slot + 2).start()
        for d in range(2):
            sender = (y + s) % Y if d == 0 else (y + Y - s) % Y
            parts = pair((t + sender // 4 + high) % 2, d, slot, d == 0)
            for who in range(2):
                if t == 0:
                    blk[s - 1][who, d] = parts[who]
                else:
                    blk[s - 1][who, d] += parts[who]

    def last_hop():
        for d in range(2):
            hop(d, 5).wait_send()
            hop(d, 6).start()

    def antipode():
        for d in range(2):
            hop(d, 6).wait_recv()

        for side in range(2):
            @pl.when(high == side)
            def _():
                left = pair(1, 0, 6, side == 0)
                right = pair(1, 1, 6, side == 0)
                for who in range(2):
                    blk[3][who, 0] = left[who] + right[who]

    def wait_bytes(ref, sem):
        pltpu.make_async_copy(ref, ref, sem).wait()

    def quarter(xx):
        return pl.ds(pl.multiple_of(xx * QUART, QUART), QUART)

    def when_owner(g, fn):
        if OWNERS[g] == Z:
            fn()
        else:
            pl.when(z < OWNERS[g])(fn)

    def when_mirrored(fn):
        pl.when(z < 8)(fn)

    def xrs_start(g):
        for d in range(X):
            q = quarter((x + d) % X)
            if d:
                remote(blk[g].at[core, :, q, :], xa[g].at[d - 1], xs_s.at[g], xs_r.at[g], x_peer(d, core)).start()
            remote(blk[g].at[other, :, q, :], xb[g].at[d], xt_s.at[g], xt_r.at[g], x_peer(d, other)).start()

    def tile(ref, g, zz, first=0):
        sign, k, row = tile_of(g, zz)
        return ref.at[k, sign, pl.ds(pl.multiple_of(first + row, TILE[g]), TILE[g]), :]

    def zrs_start(g):
        wait_bytes(xa[g], xs_r.at[g])
        wait_bytes(xb[g], xt_r.at[g])
        xs[g][core] = (blk[g][core, :, quarter(x), :] + xa[g][0]) + (xa[g][1] + xa[g][2])
        xs[g][other] = (xb[g][0] + xb[g][1]) + (xb[g][2] + xb[g][3])

        @pl.loop(1, Z)
        def _(d):
            zz = (z + d) % Z

            def send():
                remote(tile(xs[g], g, zz), zr[g].at[d - 1], zs_s.at[g], zs_r.at[g], z_peer(d)).start()

            if OWNERS[g] == Z:
                send()
            else:
                pl.when(zz < OWNERS[g])(send)

    def exchange(g):
        return remote(zt[g], ze[g], e_s.at[g], e_r.at[g], mirror(g))

    def ex_start(g):
        def collect():
            wait_bytes(zr[g], zs_r.at[g])
            total = tile(xs[g], g, z)[...]
            for d in range(Z - 1):
                total = total + zr[g][d]
            zt[g][...] = total

        when_owner(g, collect)
        when_mirrored(lambda: exchange(g).start())

    def zag_start(g):
        @pl.when(z < 8)
        def _():
            exchange(g).wait_recv()
            tile(full[g], g, z, x * QUART)[...] = zt[g][...] + ze[g][...]

        if g == 0:
            @pl.when(z >= 8)
            def _():
                tile(full[g], g, z, x * QUART)[...] = zt[g][...]

        def spread_out():
            @pl.loop(1, Z)
            def _(d):
                mine = tile(full[g], g, z, x * QUART)
                remote(mine, mine, zg_s.at[g], zg_r.at[g], z_peer(d)).start()

        when_owner(g, spread_out)

    def x_slab(g):
        return full[g].at[:, :, quarter(x), :]

    def three_quarters(g):
        return full[g].at[:, :, pl.ds(0, 3 * QUART), :]

    def xag_start(g):
        if OWNERS[g] == Z:
            wait_bytes(zr[g], zg_r.at[g])
        else:
            @pl.when(z < OWNERS[g])
            def _():
                wait_bytes(zr[g].at[pl.ds(0, OWNERS[g] - 1)], zg_r.at[g])

            @pl.when(z >= OWNERS[g])
            def _():
                wait_bytes(zr[g].at[pl.ds(0, OWNERS[g])], zg_r.at[g])
        for d in range(1, X):
            remote(x_slab(g), x_slab(g), xg_s.at[g], xg_r.at[g], x_peer(d, core)).start()

    def put(d, k, value):
        out_ref[:, pl.ds(pl.multiple_of((2 * d + k) * BLK, BLK), BLK)] = value

    def finish(g):
        wait_bytes(three_quarters(g), xg_r.at[g])
        s = g + 1
        if g < 3:
            for k in range(2):
                put((y + s) % Y, k, full[g][k, 0])
                put((y + Y - s) % Y, k, full[g][k, 1].T)
                if g == 0:
                    put(y, k, full[g][k, 2])
        else:
            for side in range(2):
                @pl.when(high == side)
                def _():
                    for k in range(2):
                        v = full[g][k, 0]
                        put((y + 4) % Y, k, v if side == 0 else v.T)

    tell(0)
    hear(0)
    tell(1)
    ring_step(1, 0)
    hear(1)
    tell(2)
    ring_step(1, 1)
    xrs_start(0)
    ring_step(2, 0)
    hear(2)
    zrs_start(0)
    ring_step(2, 1)
    xrs_start(1)
    ring_step(3, 0)
    ex_start(0)
    zrs_start(1)
    last_hop()
    ring_step(3, 1)
    xrs_start(2)
    zag_start(0)
    antipode()
    xrs_start(3)
    ex_start(1)
    zrs_start(2)
    xag_start(0)
    zag_start(1)
    zrs_start(3)
    ex_start(2)
    xag_start(1)
    zag_start(2)
    ex_start(3)
    finish(0)
    zag_start(3)
    finish(1)
    xag_start(2)
    xag_start(3)
    finish(2)
    finish(3)

    for t in range(2):
        for d in range(2):
            to_partner(t, d).wait_send()
    for d in range(2):
        for slot in (0, 1, 2, 3, 4, 6):
            hop(d, slot).wait_send()
    for g in range(GROUPS):
        wait_bytes(xa[g], xs_s.at[g])
        wait_bytes(xb[g], xt_s.at[g])
        if OWNERS[g] == Z:
            wait_bytes(zr[g], zs_s.at[g])
            wait_bytes(zr[g], zg_s.at[g])
        else:
            @pl.when(z < OWNERS[g])
            def _():
                wait_bytes(zr[g].at[pl.ds(0, OWNERS[g] - 1)], zs_s.at[g])
                wait_bytes(zr[g], zg_s.at[g])

            @pl.when(z >= OWNERS[g])
            def _():
                wait_bytes(zr[g].at[pl.ds(0, OWNERS[g])], zs_s.at[g])
        when_mirrored(lambda: exchange(g).wait_send())
        wait_bytes(three_quarters(g), xg_s.at[g])


def on_device(three_centre, screening, coefficients, occ_pattern):
    nocc = coefficients.shape[1]
    norb = coefficients.shape[0]
    bf, f32 = jnp.bfloat16, jnp.float32
    dma = pltpu.SemaphoreType.DMA
    vmem = pltpu.VMEM
    nslices = occ_pattern.shape[1]
    switches = jnp.concatenate(
        [occ_pattern, jnp.pad(screening[:, 0, :], ((0, 4), (0, nslices - screening.shape[2])))], axis=0)
    return pl.pallas_call(
        kernel,
        out_shape=jax.ShapeDtypeStruct((BLK, norb), f32),
        in_specs=[pl.BlockSpec(memory_space=pl.ANY)] * 2 + [pl.BlockSpec(memory_space=vmem)],
        out_specs=pl.BlockSpec(memory_space=vmem),
        scratch_shapes=[
            vmem((4, BLK, norb), bf),
            vmem((norb, nocc), bf),
            vmem((2, 2, 2, BLK, nocc), bf),
            vmem((2, 7, BLK, nocc), bf),
            *[vmem((2, n, BLK, BLK), f32) for n in SIGNS],
            *[vmem((X - 1, n, QUART, BLK), f32) for n in SIGNS],
            *[vmem((X, n, QUART, BLK), f32) for n in SIGNS],
            *[vmem((2, n, QUART, BLK), f32) for n in SIGNS],
            *[vmem((Z - 1, r, BLK), f32) for r in TILE],
            *[vmem((r, BLK), f32) for r in TILE],
            *[vmem((r, BLK), f32) for r in TILE],
            *[vmem((2, n, BLK, BLK), f32) for n in SIGNS],
            dma((8,)),
            dma((2, 2)), dma((2, 2)),
            dma((2, 7)), dma((2, 7)),
            *[dma((GROUPS,))] * 12,
            pltpu.SemaphoreType.REGULAR((3,)),
        ],
        compiler_params=pltpu.CompilerParams(
            collective_id=0, has_side_effects=True, vmem_limit_bytes=52 * 2**20),
        cost_estimate=pl.CostEstimate(flops=3 * 10**9, bytes_accessed=6 * 10**6, transcendentals=0),
    )(three_centre, coefficients, switches)


def solution(mesh):
    return jax.shard_map(
        on_device,
        mesh=mesh,
        in_specs=(P("aux", "orb", None), P("aux", "orb", None), P(), P()),
        out_specs=P("orb", None),
        check_vma=False,
    )
```
